256 devices in a mesh: pipe: 8 (over z), expert: 32 (over x, y, core).
Axes of the slice: x: 4, y: 4, z: 8, core: 2. Of those that a mesh axis runs over, the one named last changes fastest.
Arguments:
- fwd_in: bfloat16 [8, 2560, 3072], P('pipe', 'expert'), may hold values from -6 to 6
- fwd_ids: int32 [8, 2560, 2], P('pipe', 'expert'), may hold values from 0 to 7, as said below
- fwd_gate: float32 [8, 2560, 2], P('pipe', 'expert'), may hold values from 0.2 to 1
- bwd_in: bfloat16 [8, 2560, 3072], P('pipe', 'expert'), may hold values from -6 to 6
- bwd_ids: int32 [8, 2560, 2], P('pipe', 'expert'), may hold values from 0 to 7, as said below
- bwd_gate: float32 [8, 2560, 2], P('pipe', 'expert'), may hold values from 0.2 to 1
- bwd_grad: bfloat16 [8, 2560, 3072], P('pipe', 'expert'), may hold values from -6 to 6
- norm_gain: float32 [8, 3072], P('pipe'), may hold values from 0.1 to 1.9
- w_up: bfloat16 [8, 3072, 8192], P('pipe', None, 'expert'), may hold values from -0.109375 to 0.109375
- w_down: bfloat16 [8, 8192, 3072], P('pipe', 'expert'), may hold values from -0.0625 to 0.0625
Outputs:
- fwd_out: bfloat16 [8, 2560, 3072], P('pipe', 'expert')
- bwd_out: bfloat16 [8, 2560, 3072], P('pipe', 'expert')
- grad_up: bfloat16 [8, 3072, 8192], P('pipe', None, 'expert')
- grad_down: bfloat16 [8, 8192, 3072], P('pipe', 'expert')
The draws below stay inside these ranges and needn't reach their ends.
Inputs may be any that keep to these rules, and one draw needn't show every extreme that they name: `fwd_ids`: each token names two different experts of 8; in each layer the 80 tokens of one device name expert 0 at most 25 times, and in each layer some device names it exactly 25 times. `bwd_ids`: as for fwd_ids.
All inputs are finite; a program needn't handle non-finite values.
Results may differ from the reference program's by a relative error of at most 0.009.
Values may be sent and summed in bfloat16 or wider, within the bound.
No kernel may reach another device: no remote copies, remote signals or barrier semaphores. Data moves between devices by JAX's collectives and lax.ppermute only.
A program may use at most 128 MiB of HBM per device.

```python
import jax
import jax.numpy as jnp
from jax import lax

D = 3072
FF = 8192
EXPERTS = 8
TOK_DEV = 80
CAP = 25
TOKENS = 2560
LAYERS = 8
N_EXPERT = 32


def route_ids(key):
    blocks = LAYERS * N_EXPERT
    keys = jax.random.split(key, 6)
    counts = jax.random.randint(keys[0], (blocks,), CAP // 4, CAP + 1)
    full_block = jax.random.randint(keys[1], (LAYERS,), 0, N_EXPERT)
    is_full = (jnp.arange(N_EXPERT, dtype=jnp.int32)[None, :] == full_block[:, None]).reshape(-1)
    counts = jnp.where(is_full, CAP, counts)
    scores = jax.random.randint(keys[2], (blocks, TOK_DEV), 0, 2 ** 20) * TOK_DEV + jnp.arange(TOK_DEV, dtype=jnp.int32)[None, :]
    ranks = jnp.argsort(jnp.argsort(scores, axis=1), axis=1)
    takes_zero = ranks < counts[:, None]
    first = jax.random.randint(keys[3], (blocks, TOK_DEV), 1, EXPERTS)
    offset = jax.random.randint(keys[4], (blocks, TOK_DEV), 1, EXPERTS - 1)
    second = (first - 1 + offset) % (EXPERTS - 1) + 1
    side = jax.random.randint(keys[5], (blocks, TOK_DEV), 0, 2)
    zeros = jnp.zeros_like(first)
    column_one = jnp.where(takes_zero, jnp.where(side == 0, zeros, first), first)
    column_two = jnp.where(takes_zero, jnp.where(side == 0, first, zeros), second)
    both = jnp.stack([column_one, column_two], axis=-1)
    return both.reshape(LAYERS, TOKENS, 2).astype(jnp.int32)


def draw_fwd_ids(key, part):
    return route_ids(jax.random.fold_in(key, 11))


def draw_bwd_ids(key, part):
    return route_ids(jax.random.fold_in(key, 23))


def block_scale(stream_key, extent, pieces, smallest, high):
    level, own = 1.0, jax.random.fold_in(stream_key, 6)
    for position, shards_of in pieces:
        steps = jnp.exp(jax.random.uniform(jax.random.fold_in(own, position), (shards_of,), jnp.float32, smallest / len(pieces), high / len(pieces)))
        level = level * jnp.repeat(steps, extent[position] // shards_of).reshape([-1 if axis == position else 1 for axis in range(len(extent))])
    return level


def centred(rng, extent, deviation, limit, pieces=(), kind=jnp.bfloat16):
    result = jax.random.normal(rng, extent, jnp.float32) * deviation
    if len(pieces) > 0:
        result = block_scale(rng, extent, pieces, -0.22, 0.18) * result
    return jnp.clip(result, min=-limit, max=limit).astype(kind)


def setup_inputs(seed: int = 0) -> dict:
    splits = jax.random.split(jax.random.key(seed), 11)
    return {
        "fwd_in": centred(splits[0], (LAYERS, TOKENS, D), 1.0, 6.0, ((0, 8), (1, 32))),
        "fwd_ids": draw_fwd_ids(jax.random.fold_in(splits[10], 71), 0),
        "fwd_gate": jnp.clip(0.2 + 0.8 * jax.random.uniform(splits[2], (LAYERS, TOKENS, 2), jnp.float32) ** block_scale(splits[2], (LAYERS, TOKENS, 2), ((0, 8), (1, 32)), -0.2, 0.2), 0.2, 1.0),
        "bwd_in": centred(splits[3], (LAYERS, TOKENS, D), 1.0, 6.0, ((0, 8), (1, 32))),
        "bwd_ids": draw_bwd_ids(jax.random.fold_in(splits[10], 71), 0),
        "bwd_gate": jnp.clip(0.2 + 0.8 * jax.random.uniform(splits[5], (LAYERS, TOKENS, 2), jnp.float32) ** block_scale(splits[5], (LAYERS, TOKENS, 2), ((0, 8), (1, 32)), -0.2, 0.2), 0.2, 1.0),
        "bwd_grad": centred(splits[6], (LAYERS, TOKENS, D), 1.0, 6.0, ((0, 8), (1, 32))),
        "norm_gain": jnp.clip(1.0 + 0.18 * jax.random.normal(splits[7], (LAYERS, D), jnp.float32), 0.1, 1.9),
        "w_up": centred(splits[8], (LAYERS, D, FF), D ** -0.5, 0.109375, ((0, 8), (2, 32))),
        "w_down": centred(splits[9], (LAYERS, FF, D), FF ** -0.5, 0.0625, ((0, 8), (1, 32))),
    }


def normal_f32(values, gain_row):
    floats = values.astype(jnp.float32)
    scale = lax.rsqrt(lax.optimization_barrier(jnp.mean(floats * floats, axis=-1, keepdims=True)) + 1e-05)
    return floats * scale * gain_row

def token_places(expert_ids):
    hits = lax.optimization_barrier(jnp.sum((expert_ids == 0).astype(jnp.int32), axis=1))
    per_source = hits.reshape(N_EXPERT, TOK_DEV)
    earlier = jnp.cumsum(per_source, axis=1) - per_source
    base = jnp.arange(N_EXPERT, dtype=jnp.int32)[:, None] * CAP
    places = jnp.where(per_source > 0, base + earlier, N_EXPERT * CAP)
    return places.reshape(-1).astype(jnp.int32)

def place_rows(rows, places):
    grid = jnp.zeros((N_EXPERT * CAP + 1, D), jnp.bfloat16).at[places].set(rows)
    return grid[:N_EXPERT * CAP]

def pick_rows(grid, places):
    padded = jnp.concatenate([grid, jnp.zeros((1, D), grid.dtype)], axis=0)
    return padded[places]

def sliced_sum(left, right):
    group = FF // N_EXPERT

    def add_group(total, index):
        left_part = lax.dynamic_slice_in_dim(left, index * group, group, 1)
        right_part = lax.dynamic_slice_in_dim(right, index * group, group, 0)
        term = jnp.dot(left_part, right_part, preferred_element_type=jnp.float32).astype(jnp.bfloat16)
        term = lax.optimization_barrier(term)
        return (total + term.astype(jnp.float32), None)
    start = jnp.zeros((left.shape[0], right.shape[1]), jnp.float32)
    total, unused = lax.scan(add_group, start, jnp.arange(N_EXPERT, dtype=jnp.int32))
    return total

def gate_weight(expert_ids, gates):
    return lax.optimization_barrier(jnp.sum(jnp.where(expert_ids == 0, gates, jnp.zeros_like(gates)), axis=1))

def segment_work(segment_args):
    x_fwd, ids_fwd, gate_fwd, x_bwd, ids_bwd, gate_bwd, grad_bwd, gain_row, up_proj, down_proj = segment_args
    places_a = token_places(ids_fwd)
    weight_a = gate_weight(ids_fwd, gate_fwd)
    u_fwd = normal_f32(x_fwd, gain_row).astype(jnp.bfloat16)
    rows_a = place_rows(u_fwd, places_a)
    pre_a = jnp.dot(rows_a, up_proj, preferred_element_type=jnp.float32)
    hidden_a = (pre_a * jax.nn.sigmoid(pre_a)).astype(jnp.bfloat16)
    expert_a = sliced_sum(hidden_a, down_proj).astype(jnp.bfloat16)
    picked_a = pick_rows(expert_a, places_a).astype(jnp.float32)
    y_fwd = (x_fwd.astype(jnp.float32) + weight_a[:, None] * picked_a).astype(jnp.bfloat16)
    places_b = token_places(ids_bwd)
    weight_b = gate_weight(ids_bwd, gate_bwd)
    u_bwd = normal_f32(x_bwd, gain_row).astype(jnp.bfloat16)
    rows_b = place_rows(u_bwd, places_b)
    scaled = (weight_b[:, None] * grad_bwd.astype(jnp.float32)).astype(jnp.bfloat16)
    grid_b = place_rows(scaled, places_b)
    pre_b = jnp.dot(rows_b, up_proj, preferred_element_type=jnp.float32)
    sigmoid_pre = jax.nn.sigmoid(pre_b)
    hidden_b = (pre_b * sigmoid_pre).astype(jnp.bfloat16)
    grad_down = jnp.dot(hidden_b.T, grid_b, preferred_element_type=jnp.float32).astype(jnp.bfloat16)
    hidden_grad = jnp.dot(grid_b, down_proj.T, preferred_element_type=jnp.float32)
    pre_grad = (hidden_grad * sigmoid_pre * (1.0 + pre_b * (1.0 - sigmoid_pre))).astype(jnp.bfloat16)
    grad_up = jnp.dot(rows_b.T, pre_grad, preferred_element_type=jnp.float32).astype(jnp.bfloat16)
    ugrad = sliced_sum(pre_grad, up_proj.T).astype(jnp.bfloat16)
    u_grad = pick_rows(ugrad, places_b).astype(jnp.float32)
    unused, pullback = jax.vjp(lambda floats: normal_f32(floats, gain_row), x_bwd.astype(jnp.float32))
    dx_bwd = (grad_bwd.astype(jnp.float32) + pullback(u_grad)[0]).astype(jnp.bfloat16)
    return (y_fwd, dx_bwd, grad_up, grad_down)

def reference(fwd_in, fwd_ids, fwd_gate, bwd_in, bwd_ids, bwd_gate, bwd_grad, norm_gain, w_up, w_down):
    y_all, dx_all, grad_up, grad_down = lax.map(segment_work, (fwd_in, fwd_ids, fwd_gate, bwd_in, bwd_ids, bwd_gate, bwd_grad, norm_gain, w_up, w_down))
    fwd_out = jnp.roll(y_all, 1, axis=0)
    bwd_out = jnp.roll(dx_all, -1, axis=0)
    return (fwd_out, bwd_out, grad_up, grad_down)
```

```python
import jax
import jax.numpy as jnp
from jax import lax
from jax.experimental import pallas as pl
from jax.experimental.pallas import tpu as pltpu
from jax.sharding import Mesh, PartitionSpec as P

BF16 = jnp.bfloat16
F32 = jnp.float32
EPS = 1e-05
N_A = 13
N_B = 12
PAD = 16
SLOTS = 2 * PAD
GATH = 40
ROWS_A = 56
ROWS_B = 48


def shift(value, axis, by):
    count = lax.axis_size(axis)
    return lax.ppermute(value, axis, [(i, (i + by) % count) for i in range(count)])


def call(kernel, outs, name):
    return pl.pallas_call(
        kernel,
        out_shape=outs,
        name=name,
        compiler_params=pltpu.CompilerParams(vmem_limit_bytes=48 * 1024 * 1024),
    )


def out(shape, dtype=BF16):
    return jax.ShapeDtypeStruct(shape, dtype)


def iota(shape, dim):
    return lax.broadcasted_iota(jnp.int32, shape, dim)


def mm(a, b, dims=((1,), (0,)), precision=None):
    return lax.dot_general(a, b, (dims, ((), ())), preferred_element_type=F32, precision=precision)


def slots_of(ids):
    tokens = ids.shape[0]
    hit = jnp.where((ids[:, 0:1] == 0) | (ids[:, 1:2] == 0), 1.0, 0.0)
    hits = jnp.broadcast_to(hit, (tokens, SLOTS))
    lower = jnp.where(iota((tokens, tokens), 0) > iota((tokens, tokens), 1), 1.0, 0.0)
    slot = mm(lower.astype(BF16), hits.astype(BF16))
    place = jnp.where(slot > N_A - 0.5, slot + (PAD - N_A), slot)
    lane = iota((tokens, SLOTS), 1).astype(F32)
    return jnp.where((hits > 0.5) & (place == lane), 1.0, 0.0)


def weights_of(ids, gates, chosen):
    gate = jnp.sum(jnp.where(ids == 0, gates, 0.0), axis=1, keepdims=True)
    wide = jnp.broadcast_to(gate, (ids.shape[0], 128))
    return mm(chosen, wide, ((0,), (0,)), lax.Precision.HIGHEST)


def pack_kernel(
    xf, idf, gf, xb, idb, gb, grad, gain, send_a, send_b, ship_f, ship_b, keep_f, keep_x, keep_g, keep_w
):
    d = xf.shape[1]
    chosen_f = slots_of(idf[...])
    chosen_b = slots_of(idb[...])
    one_f = chosen_f.astype(BF16)
    one_b = chosen_b.astype(BF16)
    weight_f = weights_of(idf[...], gf[...], chosen_f)
    weight_b = weights_of(idb[...], gb[...], chosen_b)
    rows_f = mm(one_f, xf[...], ((0,), (0,)))
    rows_x = mm(one_b, xb[...], ((0,), (0,)))
    rows_g = mm(one_b, grad[...], ((0,), (0,)))

    def normal(rows):
        scale = lax.rsqrt(jnp.mean(rows * rows, axis=-1, keepdims=True) + EPS)
        return (rows * scale * gain[...]).astype(BF16)

    scaled = (rows_g * weight_b[:, 0:1]).astype(BF16)
    stacked = jnp.concatenate([normal(rows_f), normal(rows_x), scaled], axis=0)
    row, col = iota((2 * GATH, 3 * SLOTS), 0), iota((2 * GATH, 3 * SLOTS), 1)
    pick = jnp.zeros((2 * GATH, 3 * SLOTS), F32)
    for k in range(3):
        slot = col - SLOTS * k
        in_a = (slot >= 0) & (slot < N_A) & (row == slot + N_A * k)
        in_b = (slot >= PAD) & (slot < PAD + N_B) & (row == slot - PAD + N_B * k + GATH)
        pick = jnp.where(in_a | in_b, 1.0, pick)
    packed = mm(pick.astype(BF16), stacked)
    send_a[...] = packed[:GATH].astype(BF16)
    send_b[...] = packed[GATH:].astype(BF16)
    keep_f[...] = rows_f.astype(BF16)
    keep_x[...] = rows_x.astype(BF16)
    keep_g[...] = rows_g.astype(BF16)
    keep_w[...] = weight_f
    ship_f[:, :d] = xf[...]
    ship_b[:, :d] = grad[...]
    pad = jnp.zeros((xf.shape[0], 128 - SLOTS), BF16)
    ship_f[:, d:] = jnp.concatenate([one_f, pad], axis=1)
    ship_b[:, d:] = jnp.concatenate([one_b, pad], axis=1)


def merge_rows(blocks, used, total):
    d = blocks[0].shape[1]
    stacked = jnp.concatenate([b[...] for b in blocks], axis=0)
    shape = (3 * total, 4 * GATH)
    row, col = iota(shape, 0), iota(shape, 1)
    pick = jnp.zeros(shape, F32)
    for k in range(3):
        for j in range(4):
            local = row - total * k - used * j
            good = (local >= 0) & (local < used) & (col == local + GATH * j + used * k)
            pick = jnp.where(good, 1.0, pick)
    moved = mm(pick.astype(BF16), stacked).astype(BF16)
    return [moved[total * k : total * (k + 1)] for k in range(3)], d


def merge_kernel(a0, a1, a2, a3, b0, b1, b2, b3, big_a, big_b):
    parts, d = merge_rows((a0, a1, a2, a3), N_A, ROWS_A)
    for k in range(3):
        big_a[:, k * d : (k + 1) * d] = parts[k]
    parts, d = merge_rows((b0, b1, b2, b3), N_B, ROWS_B)
    for k in range(3):
        big_b[:, k * d : (k + 1) * d] = parts[k]


def down_kernel(hid, pg, wd0, wd1, wu0, wu1, *blocks):
    half = wd0.shape[0]
    hidden, grad = hid[...], pg[...]
    first = mm(hidden[:, :half], wd0[...]) + mm(hidden[:, half:], wd1[...])
    second = mm(grad[:, :half], wu0[...], ((1,), (1,))) + mm(grad[:, half:], wu1[...], ((1,), (1,)))
    start = 0
    for block in blocks:
        rows = block.shape[0] // 2
        block[:rows] = first[start : start + rows].astype(BF16)
        block[rows:] = second[start : start + rows].astype(BF16)
        start += rows


def down(hidden, pgrad, wd0, wd1, wu0, wu1):
    rows, width = hidden.shape
    half, d = wd0.shape
    tile = 512
    counts = [ROWS_A] * 4 + [ROWS_B] * 4
    whole = pl.BlockSpec((rows, width), lambda i: (0, 0))
    down_spec = pl.BlockSpec((half, tile), lambda i: (0, i))
    up_spec = pl.BlockSpec((tile, half), lambda i: (i, 0))
    return pl.pallas_call(
        down_kernel,
        grid=(d // tile,),
        in_specs=[whole, whole, down_spec, down_spec, up_spec, up_spec],
        out_specs=[pl.BlockSpec((2 * n, tile), lambda i: (0, i)) for n in counts],
        out_shape=[out((2 * n, d)) for n in counts],
        name="down",
        compiler_params=pltpu.CompilerParams(vmem_limit_bytes=48 * 1024 * 1024),
    )(hidden, pgrad, wd0, wd1, wu0, wu1)


def sum_rows(blocks, used, total):
    acc = blocks[0][...].astype(F32)
    for b in blocks[1:]:
        acc = acc + b[...].astype(F32)
    shape = (4 * SLOTS, 2 * total)
    row, col = iota(shape, 0), iota(shape, 1)
    pick = jnp.zeros(shape, F32)
    for j in range(4):
        for k in range(2):
            slot = row - SLOTS * j - PAD * k
            good = (slot >= 0) & (slot < used) & (col == slot + used * j + total * k)
            pick = jnp.where(good, 1.0, pick)
    moved = mm(pick.astype(BF16), acc.astype(BF16)).astype(BF16)
    return [moved[SLOTS * j : SLOTS * (j + 1)] for j in range(4)]


def sum_kernel(a0, a1, a2, a3, b0, b1, b2, b3, *outs):
    parts = sum_rows((a0, a1, a2, a3), N_A, ROWS_A) + sum_rows((b0, b1, b2, b3), N_B, ROWS_B)
    for ref, part in zip(outs, parts):
        ref[...] = part


def rows_kernel(a0, a1, a2, a3, b0, b1, b2, b3, keep_f, keep_x, keep_g, keep_w, gain, y_rows, dx_rows):
    def total(refs):
        acc = refs[0][...].astype(F32)
        for r in refs[1:]:
            acc = acc + r[...].astype(F32)
        return acc.astype(BF16).astype(F32)

    part_a, part_b = total((a0, a1, a2, a3)), total((b0, b1, b2, b3))
    expert = jnp.concatenate([part_a[:PAD], part_b[:PAD]], axis=0)
    du = jnp.concatenate([part_a[PAD:], part_b[PAD:]], axis=0)
    y = keep_f[...].astype(F32) + keep_w[:, 0:1] * expert
    y_rows[...] = y.astype(BF16)
    x = keep_x[...].astype(F32)
    scale = lax.rsqrt(jnp.mean(x * x, axis=-1, keepdims=True) + EPS)
    h = du * gain[...]
    inner = jnp.mean(h * x, axis=-1, keepdims=True)
    dx = scale * h - x * (scale * scale * scale * inner)
    dx_rows[...] = (keep_g[...].astype(F32) + dx).astype(BF16)


def place_kernel(ship_f, y_rows, ship_b, dx_rows, y_out, dx_out):
    d = y_rows.shape[1]
    for ship, rows, result in ((ship_f, y_rows, y_out), (ship_b, dx_rows, dx_out)):
        chosen = ship[:, d:][:, :SLOTS]
        hit = jnp.sum(chosen.astype(F32), axis=1, keepdims=True)
        placed = mm(chosen, rows[...])
        result[...] = jnp.where(hit > 0.5, placed, ship[:, :d].astype(F32)).astype(BF16)


def ring_gather(own, axis, first):
    ahead = shift(own, axis, 1)
    behind = shift(own, axis, -1)
    far = jnp.concatenate([shift(ahead[:first], axis, 1), shift(behind[first:], axis, -1)], axis=0)
    return [own, ahead, far, behind]


def on_device(
    fwd_in, fwd_ids, fwd_gate, bwd_in, bwd_ids, bwd_gate, bwd_grad, norm_gain, w_up, w_down
):
    tokens, d = fwd_in.shape[1:]
    up_own, down_own = w_up[0], w_down[0]
    hidden_own = up_own.shape[1]
    send_a, send_b, ship_f, ship_b, keep_f, keep_x, keep_g, keep_w = call(
        pack_kernel,
        [
            out((GATH, d)),
            out((GATH, d)),
            out((tokens, d + 128)),
            out((tokens, d + 128)),
            out((SLOTS, d)),
            out((SLOTS, d)),
            out((SLOTS, d)),
            out((SLOTS, 128), F32),
        ],
        "pack",
    )(fwd_in[0], fwd_ids[0], fwd_gate[0], bwd_in[0], bwd_ids[0], bwd_gate[0], bwd_grad[0], norm_gain)
    a_blocks = [send_a, shift(send_a, "x", 1), shift(send_a, "x", 2), shift(send_a, "x", -1)]
    b_blocks = [send_b, shift(send_b, "y", 1), shift(send_b, "y", 2), shift(send_b, "y", -1)]
    big_a, big_b = call(merge_kernel, [out((ROWS_A, 3 * d)), out((ROWS_B, 3 * d))], "merge")(
        *a_blocks, *b_blocks
    )
    up_other = shift(up_own, "core", 1)
    down_other = shift(down_own, "core", 1)
    arrived_f = shift(ship_f, "pipe", 1)
    arrived_b = shift(ship_b, "pipe", -1)

    blocks = ring_gather(big_a, "y", 32) + ring_gather(big_b, "x", 24)
    rows = jnp.concatenate(blocks, axis=0)
    rows_a, rows_b, grid_b = rows[:, :d], rows[:, d : 2 * d], rows[:, 2 * d :]
    up = jnp.concatenate([up_own, up_other], axis=1)
    dn = jnp.concatenate([down_own, down_other], axis=0)
    pre_a = mm(rows_a, up)
    hidden_a = (pre_a * jax.nn.sigmoid(pre_a)).astype(BF16)
    pre_b = mm(rows_b, up)
    sigma = jax.nn.sigmoid(pre_b)
    hidden_b = (pre_b * sigma).astype(BF16)
    hidden_grad = mm(grid_b, dn, ((1,), (1,)))
    pgrad = (hidden_grad * sigma * (1.0 + pre_b * (1.0 - sigma))).astype(BF16)
    parts = down(hidden_a, pgrad, down_own, down_other, up_own, up_other)

    a_sums = [parts[0], shift(parts[1], "y", -1), shift(parts[2], "y", 2), shift(parts[3], "y", 1)]
    b_sums = [parts[4], shift(parts[5], "x", -1), shift(parts[6], "x", 2), shift(parts[7], "x", 1)]

    down_part = mm(hidden_b, grid_b, ((0,), (0,)))
    up_part = mm(rows_b, pgrad, ((0,), (0,)))
    up_theirs = shift(up_part[:, hidden_own:].astype(BF16), "core", 1)
    down_theirs = shift(down_part[hidden_own:].astype(BF16), "core", 1)
    grad_up = (up_part[:, :hidden_own] + up_theirs.astype(F32)).astype(BF16)
    grad_down = (down_part[:hidden_own] + down_theirs.astype(F32)).astype(BF16)

    q = call(sum_kernel, [out((SLOTS, d))] * 8, "sums")(*a_sums, *b_sums)
    a_last = [q[0], shift(q[1], "x", -1), shift(q[2], "x", 2), shift(q[3], "x", 1)]
    b_last = [q[4], shift(q[5], "y", -1), shift(q[6], "y", 2), shift(q[7], "y", 1)]
    y_rows, dx_rows = call(rows_kernel, [out((SLOTS, d)), out((SLOTS, d))], "rows")(
        *a_last, *b_last, keep_f, keep_x, keep_g, keep_w, norm_gain
    )
    y_arrived = shift(y_rows, "pipe", 1)
    dx_arrived = shift(dx_rows, "pipe", -1)
    fwd_out, bwd_out = call(place_kernel, [out((tokens, d)), out((tokens, d))], "place")(
        arrived_f, y_arrived, arrived_b, dx_arrived
    )
    return (fwd_out[None], bwd_out[None], grad_up[None], grad_down[None])


def solution(mesh):
    chips = Mesh(mesh.devices.reshape(8, 4, 4, 2), ("pipe", "x", "y", "core"))
    expert = ("x", "y", "core")
    tokens = P("pipe", expert, None)
    return jax.shard_map(
        on_device,
        mesh=chips,
        in_specs=(tokens,) * 7 + (P("pipe", None), P("pipe", None, expert), P("pipe", expert, None)),
        out_specs=(tokens, tokens, P("pipe", None, expert), P("pipe", expert, None)),
        check_vma=False,
    )
```

```python
import jax
import jax.numpy as jnp
from jax import lax
from jax.experimental import pallas as pl
from jax.experimental.pallas import tpu as pltpu
from jax.sharding import Mesh, PartitionSpec as P

BF16 = jnp.bfloat16
F32 = jnp.float32
EPS = 1e-05
N_A = 13
N_B = 12
PAD = 16
SLOTS = 2 * PAD
GATH = 40
ROWS_A = 56
ROWS_B = 48


def shift(value, axis, by):
    count = lax.axis_size(axis)
    return lax.ppermute(value, axis, [(i, (i + by) % count) for i in range(count)])


def call(kernel, outs, name, vmem=20, after=None):
    count, unused = after or (0, 0)
    specs = {}
    if unused:
        whole, later = pl.BlockSpec(memory_space=pltpu.VMEM), pl.BlockSpec(memory_space=pl.ANY)
        specs = {"in_specs": [whole] * (count - unused) + [later] * unused}
    return pl.pallas_call(
        kernel,
        **specs,
        out_shape=outs,
        name=name,
        compiler_params=pltpu.CompilerParams(vmem_limit_bytes=vmem * 1000 * 1024),
    )


def out(shape, dtype=BF16):
    return jax.ShapeDtypeStruct(shape, dtype)


def iota(shape, dim):
    return lax.broadcasted_iota(jnp.int32, shape, dim)


def mm(a, b, dims=((1,), (0,)), precision=None):
    return lax.dot_general(a, b, (dims, ((), ())), preferred_element_type=F32, precision=precision)


def slots_of(ids):
    tokens = ids.shape[1]
    hit = jnp.where((ids[0:1] == 0) | (ids[1:2] == 0), 1.0, 0.0)
    hits = jnp.broadcast_to(hit, (SLOTS, tokens))
    before = jnp.where(iota((tokens, tokens), 0) < iota((tokens, tokens), 1), 1.0, 0.0)
    slot = mm(hits.astype(BF16), before.astype(BF16))
    place = jnp.where(slot > N_A - 0.5, slot + (PAD - N_A), slot)
    return jnp.where((hits > 0.5) & (place == iota((SLOTS, tokens), 0).astype(F32)), 1.0, 0.0)


def weights_of(ids, gates, chosen):
    gate = jnp.sum(jnp.where(ids == 0, gates, 0.0), axis=0, keepdims=True)
    return jnp.sum(chosen * gate, axis=1, keepdims=True)


def pack_kernel(
    xf, idf, gf, xb, idb, gb, grad, gain, send_a, send_b, keep_f, keep_x, keep_g, keep_w, place_f, place_b
):
    chosen_f = slots_of(idf[...])
    chosen_b = slots_of(idb[...])
    one_f = chosen_f.astype(BF16)
    one_b = chosen_b.astype(BF16)
    weight_f = weights_of(idf[...], gf[...], chosen_f)
    weight_b = weights_of(idb[...], gb[...], chosen_b)
    rows_f = mm(one_f, xf[...])
    rows_x = mm(one_b, xb[...])
    rows_g = mm(one_b, grad[...])

    def normal(rows):
        scale = lax.rsqrt(jnp.mean(rows * rows, axis=-1, keepdims=True) + EPS)
        return (rows * scale * gain[...]).astype(BF16)

    scaled = (rows_g * weight_b).astype(BF16)
    stacked = jnp.concatenate([normal(rows_f), normal(rows_x), scaled], axis=0)
    row, col = iota((2 * GATH, 3 * SLOTS), 0), iota((2 * GATH, 3 * SLOTS), 1)
    pick = jnp.zeros((2 * GATH, 3 * SLOTS), F32)
    for k in range(3):
        slot = col - SLOTS * k
        in_a = (slot >= 0) & (slot < N_A) & (row == slot + N_A * k)
        in_b = (slot >= PAD) & (slot < PAD + N_B) & (row == slot - PAD + N_B * k + GATH)
        pick = jnp.where(in_a | in_b, 1.0, pick)
    packed = mm(pick.astype(BF16), stacked)
    send_a[...] = packed[:GATH].astype(BF16)
    send_b[...] = packed[GATH:].astype(BF16)
    keep_f[...] = rows_f.astype(BF16)
    keep_x[...] = rows_x.astype(BF16)
    keep_g[...] = rows_g.astype(BF16)
    keep_w[...] = jnp.broadcast_to(weight_f, keep_w.shape)
    pad = jnp.zeros((SLOTS, 128 - xf.shape[0]), BF16)
    place_f[...] = jnp.concatenate([one_f, pad], axis=1)
    place_b[...] = jnp.concatenate([one_b, pad], axis=1)


def merge_rows(blocks, used, total):
    d = blocks[0].shape[1]
    stacked = jnp.concatenate([b[...] for b in blocks], axis=0)
    shape = (3 * total, 4 * GATH)
    row, col = iota(shape, 0), iota(shape, 1)
    pick = jnp.zeros(shape, F32)
    for k in range(3):
        for j in range(4):
            local = row - total * k - used * j
            good = (local >= 0) & (local < used) & (col == local + GATH * j + used * k)
            pick = jnp.where(good, 1.0, pick)
    moved = mm(pick.astype(BF16), stacked).astype(BF16)
    return [moved[total * k : total * (k + 1)] for k in range(3)], d


def merge_kernel(a0, a1, a2, a3, b0, b1, b2, b3, big_a, big_b):
    parts, d = merge_rows((a0, a1, a2, a3), N_A, ROWS_A)
    for k in range(3):
        big_a[:, k * d : (k + 1) * d] = parts[k]
    parts, d = merge_rows((b0, b1, b2, b3), N_B, ROWS_B)
    for k in range(3):
        big_b[:, k * d : (k + 1) * d] = parts[k]


def down_kernel(hid, pg, dn, up, after_f, after_b, *blocks):
    first = mm(hid[...], dn[...])
    second = mm(pg[...], up[...])
    start = 0
    for block in blocks:
        rows = block.shape[0] // 2
        block[:rows] = first[start : start + rows].astype(BF16)
        block[rows:] = second[start : start + rows].astype(BF16)
        start += rows


def down(hidden, pgrad, dn, up, *after):
    rows, width = hidden.shape
    d = dn.shape[1]
    tile = 768
    counts = [ROWS_A] * 4 + [ROWS_B] * 4
    whole = pl.BlockSpec((rows, width), lambda i: (0, 0))
    spec = pl.BlockSpec((width, tile), lambda i: (0, i))
    return pl.pallas_call(
        down_kernel,
        grid=(d // tile,),
        in_specs=[whole, whole, spec, spec] + [pl.BlockSpec(memory_space=pl.ANY)] * len(after),
        out_specs=[pl.BlockSpec((2 * n, tile), lambda i: (0, i)) for n in counts],
        out_shape=[pltpu.HBM((2 * n, d), BF16) for n in counts],
        name="down",
        compiler_params=pltpu.CompilerParams(vmem_limit_bytes=16 * 1000 * 1024),
    )(hidden, pgrad, dn, up, *after)


def sum_rows(blocks, used, total):
    acc = blocks[0][...].astype(F32)
    for b in blocks[1:]:
        acc = acc + b[...].astype(F32)
    shape = (4 * SLOTS, 2 * total)
    row, col = iota(shape, 0), iota(shape, 1)
    pick = jnp.zeros(shape, F32)
    for j in range(4):
        for k in range(2):
            slot = row - SLOTS * j - PAD * k
            good = (slot >= 0) & (slot < used) & (col == slot + used * j + total * k)
            pick = jnp.where(good, 1.0, pick)
    moved = mm(pick.astype(BF16), acc.astype(BF16)).astype(BF16)
    return [moved[SLOTS * j : SLOTS * (j + 1)] for j in range(4)]


def sum_kernel(a0, a1, a2, a3, b0, b1, b2, b3, kept_up, kept_down, *outs):
    parts = sum_rows((a0, a1, a2, a3), N_A, ROWS_A) + sum_rows((b0, b1, b2, b3), N_B, ROWS_B)
    for ref, part in zip(outs, parts):
        ref[...] = part


def sums(a_blocks, b_blocks, *kept):
    d = a_blocks[0].shape[1]
    here, there = pl.BlockSpec(memory_space=pltpu.VMEM), pl.BlockSpec(memory_space=pl.ANY)
    return pl.pallas_call(
        sum_kernel,
        in_specs=[here] * 8 + [there] * len(kept),
        out_specs=[here] * 8 + [there] * len(kept),
        out_shape=[out((SLOTS, d))] * 8 + [out(k.shape) for k in kept],
        input_output_aliases={8 + i: 8 + i for i in range(len(kept))},
        name="sums",
        compiler_params=pltpu.CompilerParams(vmem_limit_bytes=20 * 1000 * 1024),
    )(*a_blocks, *b_blocks, *kept)


def rows_kernel(
    a0, a1, a2, a3, b0, b1, b2, b3, keep_f, keep_x, keep_g, keep_w, place_f, place_b, gain, y_rows, dx_rows
):
    d = keep_f.shape[1]

    def total(refs):
        acc = refs[0][...].astype(F32)
        for r in refs[1:]:
            acc = acc + r[...].astype(F32)
        return acc.astype(BF16).astype(F32)

    part_a, part_b = total((a0, a1, a2, a3)), total((b0, b1, b2, b3))
    expert = jnp.concatenate([part_a[:PAD], part_b[:PAD]], axis=0)
    du = jnp.concatenate([part_a[PAD:], part_b[PAD:]], axis=0)
    y = keep_f[...].astype(F32) + keep_w[:, 0:1] * expert
    y_rows[:, :d] = y.astype(BF16)
    y_rows[:, d:] = place_f[...]
    x = keep_x[...].astype(F32)
    scale = lax.rsqrt(jnp.mean(x * x, axis=-1, keepdims=True) + EPS)
    h = du * gain[...]
    inner = jnp.mean(h * x, axis=-1, keepdims=True)
    dx = scale * h - x * (scale * scale * scale * inner)
    dx_rows[:, :d] = (keep_g[...].astype(F32) + dx).astype(BF16)
    dx_rows[:, d:] = place_b[...]


def place_kernel(base_f, y_rows, base_b, dx_rows, after_up, after_down, y_out, dx_out):
    tokens, d = base_f.shape
    ones = jnp.ones((SLOTS, 128), BF16)
    for base, rows, result in ((base_f, y_rows, y_out), (base_b, dx_rows, dx_out)):
        chosen = rows[:, d:]
        hit = mm(chosen, ones, ((0,), (0,)))[:tokens, 0:1]
        placed = mm(chosen, rows[:, :d], ((0,), (0,)))[:tokens]
        result[...] = jnp.where(hit > 0.5, placed, base[...].astype(F32)).astype(BF16)


def ring_gather(own, axis, first):
    ahead = shift(own, axis, 1)
    behind = shift(own, axis, -1)
    far = jnp.concatenate([shift(ahead[:first], axis, 1), shift(behind[first:], axis, -1)], axis=0)
    return [own, ahead, far, behind]


def on_device(
    fwd_in, fwd_ids, fwd_gate, bwd_in, bwd_ids, bwd_gate, bwd_grad, norm_gain, w_up, w_down
):
    tokens, d = fwd_in.shape[1:]
    hold = lax.optimization_barrier
    send_a, send_b, keep_f, keep_x, keep_g, keep_w, place_f, place_b = call(
        pack_kernel,
        [out((GATH, d))] * 2 + [out((SLOTS, d))] * 3 + [out((SLOTS, 128), F32)] + [out((SLOTS, 128))] * 2,
        "pack",
        62,
    )(
        fwd_in[0],
        fwd_ids[0].T,
        fwd_gate[0].T,
        bwd_in[0],
        bwd_ids[0].T,
        bwd_gate[0].T,
        bwd_grad[0],
        norm_gain,
    )
    send_a, send_b, up_own, down_own = hold((send_a, send_b, w_up[0], w_down[0]))
    a_blocks = [send_a, shift(send_a, "x", 1), shift(send_a, "x", 2), shift(send_a, "x", -1)]
    b_blocks = [send_b, shift(send_b, "y", 1), shift(send_b, "y", 2), shift(send_b, "y", -1)]
    up = lax.all_gather(up_own.T, "core", axis=0, tiled=True)
    dn = lax.all_gather(down_own, "core", axis=0, tiled=True)
    big_a, big_b = call(merge_kernel, [out((ROWS_A, 3 * d)), out((ROWS_B, 3 * d))], "merge")(
        *a_blocks, *b_blocks
    )
    blocks = ring_gather(big_a, "y", 32) + ring_gather(big_b, "x", 24)
    rows = jnp.concatenate(blocks, axis=0)
    rows, base_f, base_b = hold((rows, fwd_in[0], bwd_grad[0]))
    base_f, base_b = shift(base_f, "pipe", 1), shift(base_b, "pipe", -1)
    rows_a, rows_b, grid_b = rows[:, :d], rows[:, d : 2 * d], rows[:, 2 * d :]
    pre_a = mm(rows_a, up, ((1,), (1,)))
    hidden_a = (pre_a * jax.nn.sigmoid(pre_a)).astype(BF16)
    pre_b = mm(rows_b, up, ((1,), (1,)))
    sigma = jax.nn.sigmoid(pre_b)
    hidden_b = (pre_b * sigma).astype(BF16)
    hidden_grad = mm(grid_b, dn, ((1,), (1,)))
    pgrad = (hidden_grad * sigma * (1.0 + pre_b * (1.0 - sigma))).astype(BF16)
    parts = down(hidden_a, pgrad, dn, up, base_f, base_b)

    a_sums = [parts[0], shift(parts[1], "y", -1), shift(parts[2], "y", 2), shift(parts[3], "y", 1)]
    b_sums = [parts[4], shift(parts[5], "x", -1), shift(parts[6], "x", 2), shift(parts[7], "x", 1)]

    half = up.shape[0] // 2
    first = lax.axis_index("core") == 0

    def halves(value):
        low, high = value[:, :half], value[:, half:]
        return jnp.where(first, low, high), jnp.where(first, high, low)

    hidden_mine, hidden_theirs = halves(hidden_b)
    pgrad_mine, pgrad_theirs = halves(pgrad)
    over_rows = ((0,), (0,))
    down_theirs = mm(hidden_theirs, grid_b, over_rows).astype(BF16)
    up_theirs = mm(rows_b, pgrad_theirs, over_rows).astype(BF16)

    *q, up_theirs, down_theirs = sums(a_sums, b_sums, up_theirs, down_theirs)
    up_theirs, down_theirs = shift(up_theirs, "core", 1), shift(down_theirs, "core", 1)
    a_last = [q[0], shift(q[1], "x", -1), shift(q[2], "x", 2), shift(q[3], "x", 1)]
    b_last = [q[4], shift(q[5], "y", -1), shift(q[6], "y", 2), shift(q[7], "y", 1)]
    y_rows, dx_rows = call(rows_kernel, [out((SLOTS, d + 128))] * 2, "rows")(
        *a_last, *b_last, keep_f, keep_x, keep_g, keep_w, place_f, place_b, norm_gain
    )
    grad_down = (mm(hidden_mine, grid_b, over_rows) + down_theirs.astype(F32)).astype(BF16)
    grad_up = (mm(rows_b, pgrad_mine, over_rows) + up_theirs.astype(F32)).astype(BF16)
    y_arrived = shift(y_rows, "pipe", 1)
    dx_arrived = shift(dx_rows, "pipe", -1)
    fwd_out, bwd_out = call(place_kernel, [out((tokens, d)), out((tokens, d))], "place", after=(6, 2))(
        base_f, y_arrived, base_b, dx_arrived, grad_up, grad_down
    )
    return (fwd_out[None], bwd_out[None], grad_up[None], grad_down[None])


def solution(mesh):
    chips = Mesh(mesh.devices.reshape(8, 4, 4, 2), ("pipe", "x", "y", "core"))
    expert = ("x", "y", "core")
    tokens = P("pipe", expert, None)
    return jax.shard_map(
        on_device,
        mesh=chips,
        in_specs=(tokens,) * 7 + (P("pipe", None), P("pipe", None, expert), P("pipe", expert, None)),
        out_specs=(tokens, tokens, P("pipe", None, expert), P("pipe", expert, None)),
        check_vma=False,
    )
```

```python
import jax
import jax.numpy as jnp
from jax import lax
from jax.experimental import pallas as pl
from jax.experimental.pallas import tpu as pltpu
from jax.sharding import Mesh, PartitionSpec as P

BF16 = jnp.bfloat16
F32 = jnp.float32
EPS = 1e-05
N_A = 13
N_B = 12
PAD = 16
SLOTS = 2 * PAD
GATH = 40
ROWS_A = 56
ROWS_B = 48


def shift(value, axis, by):
    count = lax.axis_size(axis)
    return lax.ppermute(value, axis, [(i, (i + by) % count) for i in range(count)])


def call(kernel, outs, name, vmem=20, after=None):
    count, unused = after or (0, 0)
    specs = {}
    if unused:
        whole, later = pl.BlockSpec(memory_space=pltpu.VMEM), pl.BlockSpec(memory_space=pl.ANY)
        specs = {"in_specs": [whole] * (count - unused) + [later] * unused}
    return pl.pallas_call(
        kernel,
        **specs,
        out_shape=outs,
        name=name,
        compiler_params=pltpu.CompilerParams(vmem_limit_bytes=vmem * 1000 * 1024),
    )


def out(shape, dtype=BF16):
    return jax.ShapeDtypeStruct(shape, dtype)


def iota(shape, dim):
    return lax.broadcasted_iota(jnp.int32, shape, dim)


def mm(a, b, dims=((1,), (0,)), precision=None):
    return lax.dot_general(a, b, (dims, ((), ())), preferred_element_type=F32, precision=precision)


def after(values, others):
    n = len(values)

    def nothing(*refs):
        pass

    anywhere = pl.BlockSpec(memory_space=pl.ANY)
    return pl.pallas_call(
        nothing,
        in_specs=[anywhere] * (n + len(others)),
        out_specs=[anywhere] * n,
        out_shape=[out(v.shape, v.dtype) for v in values],
        input_output_aliases={i: i for i in range(n)},
        name="after",
        compiler_params=pltpu.CompilerParams(vmem_limit_bytes=1 << 20),
    )(*values, *others)


def slots_of(ids):
    tokens = ids.shape[1]
    hit = jnp.where((ids[0:1] == 0) | (ids[1:2] == 0), 1.0, 0.0)
    hits = jnp.broadcast_to(hit, (SLOTS, tokens))
    before = jnp.where(iota((tokens, tokens), 0) < iota((tokens, tokens), 1), 1.0, 0.0)
    slot = mm(hits.astype(BF16), before.astype(BF16))
    place = jnp.where(slot > N_A - 0.5, slot + (PAD - N_A), slot)
    return jnp.where((hits > 0.5) & (place == iota((SLOTS, tokens), 0).astype(F32)), 1.0, 0.0)


def weights_of(ids, gates, chosen):
    gate = jnp.sum(jnp.where(ids == 0, gates, 0.0), axis=0, keepdims=True)
    return jnp.sum(chosen * gate, axis=1, keepdims=True)


def pack_kernel(
    xf, idf, gf, xb, idb, gb, grad, gain, send_a, send_b, keep_f, keep_x, keep_g, keep_w, place_f, place_b, ship_f, ship_b
):
    chosen_f = slots_of(idf[...])
    chosen_b = slots_of(idb[...])
    one_f = chosen_f.astype(BF16)
    one_b = chosen_b.astype(BF16)
    weight_f = weights_of(idf[...], gf[...], chosen_f)
    weight_b = weights_of(idb[...], gb[...], chosen_b)
    rows_f = mm(one_f, xf[...])
    rows_x = mm(one_b, xb[...])
    rows_g = mm(one_b, grad[...])

    def normal(rows):
        scale = lax.rsqrt(jnp.mean(rows * rows, axis=-1, keepdims=True) + EPS)
        return (rows * scale * gain[...]).astype(BF16)

    scaled = (rows_g * weight_b).astype(BF16)
    stacked = jnp.concatenate([normal(rows_f), normal(rows_x), scaled], axis=0)
    row, col = iota((2 * GATH, 3 * SLOTS), 0), iota((2 * GATH, 3 * SLOTS), 1)
    pick = jnp.zeros((2 * GATH, 3 * SLOTS), F32)
    for k in range(3):
        slot = col - SLOTS * k
        in_a = (slot >= 0) & (slot < N_A) & (row == slot + N_A * k)
        in_b = (slot >= PAD) & (slot < PAD + N_B) & (row == slot - PAD + N_B * k + GATH)
        pick = jnp.where(in_a | in_b, 1.0, pick)
    packed = mm(pick.astype(BF16), stacked)
    send_a[...] = packed[:GATH].astype(BF16)
    send_b[...] = packed[GATH:].astype(BF16)
    keep_f[...] = rows_f.astype(BF16)
    keep_x[...] = rows_x.astype(BF16)
    keep_g[...] = rows_g.astype(BF16)
    keep_w[...] = jnp.broadcast_to(weight_f, keep_w.shape)
    pad = jnp.zeros((SLOTS, 128 - xf.shape[0]), BF16)
    place_f[...] = jnp.concatenate([one_f, pad], axis=1)
    place_b[...] = jnp.concatenate([one_b, pad], axis=1)
    ship_f[...] = xf[...]
    ship_b[...] = grad[...]


def merge_rows(blocks, used, total):
    d = blocks[0].shape[1]
    stacked = jnp.concatenate([b[...] for b in blocks], axis=0)
    shape = (3 * total, 4 * GATH)
    row, col = iota(shape, 0), iota(shape, 1)
    pick = jnp.zeros(shape, F32)
    for k in range(3):
        for j in range(4):
            local = row - total * k - used * j
            good = (local >= 0) & (local < used) & (col == local + GATH * j + used * k)
            pick = jnp.where(good, 1.0, pick)
    moved = mm(pick.astype(BF16), stacked).astype(BF16)
    return [moved[total * k : total * (k + 1)] for k in range(3)], d


def merge_kernel(a0, a1, a2, a3, b0, b1, b2, b3, after_up, after_down, big_a, big_b):
    parts, d = merge_rows((a0, a1, a2, a3), N_A, ROWS_A)
    for k in range(3):
        big_a[:, k * d : (k + 1) * d] = parts[k]
    parts, d = merge_rows((b0, b1, b2, b3), N_B, ROWS_B)
    for k in range(3):
        big_b[:, k * d : (k + 1) * d] = parts[k]


def flip_kernel(own, other, across):
    half = own.shape[1]
    across[:half] = own[...].T
    across[half:] = other[...].T


def down_kernel(hid, pg, dn, up, after_f, after_b, *blocks):
    first = mm(hid[...], dn[...])
    second = mm(pg[...], up[...])
    start = 0
    for block in blocks:
        rows = block.shape[0] // 2
        block[:rows] = first[start : start + rows].astype(BF16)
        block[rows:] = second[start : start + rows].astype(BF16)
        start += rows


def down(hidden, pgrad, dn, up, *after):
    rows, width = hidden.shape
    d = dn.shape[1]
    tile = 768
    counts = [ROWS_A] * 4 + [ROWS_B] * 4
    whole = pl.BlockSpec((rows, width), lambda i: (0, 0))
    spec = pl.BlockSpec((width, tile), lambda i: (0, i))
    return pl.pallas_call(
        down_kernel,
        grid=(d // tile,),
        in_specs=[whole, whole, spec, spec] + [pl.BlockSpec(memory_space=pl.ANY)] * len(after),
        out_specs=[pl.BlockSpec((2 * n, tile), lambda i: (0, i)) for n in counts],
        out_shape=[pltpu.HBM((2 * n, d), BF16) for n in counts],
        name="down",
        compiler_params=pltpu.CompilerParams(vmem_limit_bytes=16 * 1000 * 1024),
    )(hidden, pgrad, dn, up, *after)


def sum_rows(blocks, used, total):
    acc = blocks[0][...].astype(F32)
    for b in blocks[1:]:
        acc = acc + b[...].astype(F32)
    shape = (4 * SLOTS, 2 * total)
    row, col = iota(shape, 0), iota(shape, 1)
    pick = jnp.zeros(shape, F32)
    for j in range(4):
        for k in range(2):
            slot = row - SLOTS * j - PAD * k
            good = (slot >= 0) & (slot < used) & (col == slot + used * j + total * k)
            pick = jnp.where(good, 1.0, pick)
    moved = mm(pick.astype(BF16), acc.astype(BF16)).astype(BF16)
    return [moved[SLOTS * j : SLOTS * (j + 1)] for j in range(4)]


def sum_kernel(a0, a1, a2, a3, b0, b1, b2, b3, kept_up, kept_down, *outs):
    parts = sum_rows((a0, a1, a2, a3), N_A, ROWS_A) + sum_rows((b0, b1, b2, b3), N_B, ROWS_B)
    for ref, part in zip(outs, parts):
        ref[...] = part


def sums(a_blocks, b_blocks, *kept):
    d = a_blocks[0].shape[1]
    here, there = pl.BlockSpec(memory_space=pltpu.VMEM), pl.BlockSpec(memory_space=pl.ANY)
    return pl.pallas_call(
        sum_kernel,
        in_specs=[here] * 8 + [there] * len(kept),
        out_specs=[here] * 8 + [there] * len(kept),
        out_shape=[out((SLOTS, d))] * 8 + [out(k.shape) for k in kept],
        input_output_aliases={8 + i: 8 + i for i in range(len(kept))},
        name="sums",
        compiler_params=pltpu.CompilerParams(vmem_limit_bytes=20 * 1000 * 1024),
    )(*a_blocks, *b_blocks, *kept)


def rows_kernel(
    a0, a1, a2, a3, b0, b1, b2, b3, keep_f, keep_x, keep_g, keep_w, place_f, place_b, gain, y_rows, dx_rows
):
    d = keep_f.shape[1]

    def total(refs):
        acc = refs[0][...].astype(F32)
        for r in refs[1:]:
            acc = acc + r[...].astype(F32)
        return acc.astype(BF16).astype(F32)

    part_a, part_b = total((a0, a1, a2, a3)), total((b0, b1, b2, b3))
    expert = jnp.concatenate([part_a[:PAD], part_b[:PAD]], axis=0)
    du = jnp.concatenate([part_a[PAD:], part_b[PAD:]], axis=0)
    y = keep_f[...].astype(F32) + keep_w[:, 0:1] * expert
    y_rows[:, :d] = y.astype(BF16)
    y_rows[:, d:] = place_f[...]
    x = keep_x[...].astype(F32)
    scale = lax.rsqrt(jnp.mean(x * x, axis=-1, keepdims=True) + EPS)
    h = du * gain[...]
    inner = jnp.mean(h * x, axis=-1, keepdims=True)
    dx = scale * h - x * (scale * scale * scale * inner)
    dx_rows[:, :d] = (keep_g[...].astype(F32) + dx).astype(BF16)
    dx_rows[:, d:] = place_b[...]


def place_kernel(base_f, y_rows, base_b, dx_rows, after_up, after_down, y_out, dx_out):
    tokens, d = base_f.shape
    ones = jnp.ones((SLOTS, 128), BF16)
    for base, rows, result in ((base_f, y_rows, y_out), (base_b, dx_rows, dx_out)):
        chosen = rows[:, d:]
        hit = mm(chosen, ones, ((0,), (0,)))[:tokens, 0:1]
        placed = mm(chosen, rows[:, :d], ((0,), (0,)))[:tokens]
        result[...] = jnp.where(hit > 0.5, placed, base[...].astype(F32)).astype(BF16)


def ring_gather(own, axis, first):
    ahead = shift(own, axis, 1)
    behind = shift(own, axis, -1)
    far = jnp.concatenate([shift(ahead[:first], axis, 1), shift(behind[first:], axis, -1)], axis=0)
    return [own, ahead, far, behind]


def on_device(
    fwd_in, fwd_ids, fwd_gate, bwd_in, bwd_ids, bwd_gate, bwd_grad, norm_gain, w_up, w_down
):
    tokens, d = fwd_in.shape[1:]
    send_a, send_b, keep_f, keep_x, keep_g, keep_w, place_f, place_b, base_f, base_b = call(
        pack_kernel,
        [out((GATH, d))] * 2 + [out((SLOTS, d))] * 3 + [out((SLOTS, 128), F32)] + [out((SLOTS, 128))] * 2
        + [pltpu.HBM((tokens, d), BF16)] * 2,
        "pack",
        62,
    )(
        fwd_in[0],
        fwd_ids[0].T,
        fwd_gate[0].T,
        bwd_in[0],
        bwd_ids[0].T,
        bwd_gate[0].T,
        bwd_grad[0],
        norm_gain,
    )
    up_own, down_own = w_up[0], w_down[0]
    a_blocks = [send_a, shift(send_a, "x", 1), shift(send_a, "x", 2), shift(send_a, "x", -1)]
    b_blocks = [send_b, shift(send_b, "y", 1), shift(send_b, "y", 2), shift(send_b, "y", -1)]
    up_other, down_other = shift(up_own, "core", 1), shift(down_own, "core", 1)
    big_a, big_b = call(merge_kernel, [out((ROWS_A, 3 * d)), out((ROWS_B, 3 * d))], "merge", after=(10, 2))(
        *a_blocks, *b_blocks, up_other, down_other
    )
    blocks = ring_gather(big_a, "y", 32) + ring_gather(big_b, "x", 24)
    rows = jnp.concatenate(blocks, axis=0)
    base_f, base_b = after((base_f, base_b), (rows,))
    base_f, base_b = shift(base_f, "pipe", 1), shift(base_b, "pipe", -1)
    rows_a, rows_b, grid_b = rows[:, :d], rows[:, d : 2 * d], rows[:, 2 * d :]
    dn = jnp.concatenate([down_own, down_other], axis=0)
    up = call(flip_kernel, out((2 * up_own.shape[1], d)), "flip")(up_own, up_other)
    pre_a = mm(rows_a, up, ((1,), (1,)))
    hidden_a = (pre_a * jax.nn.sigmoid(pre_a)).astype(BF16)
    pre_b = mm(rows_b, up, ((1,), (1,)))
    sigma = jax.nn.sigmoid(pre_b)
    hidden_b = (pre_b * sigma).astype(BF16)
    hidden_grad = mm(grid_b, dn, ((1,), (1,)))
    pgrad = (hidden_grad * sigma * (1.0 + pre_b * (1.0 - sigma))).astype(BF16)
    parts = down(hidden_a, pgrad, dn, up, base_f, base_b)

    a_sums = [parts[0], shift(parts[1], "y", -1), shift(parts[2], "y", 2), shift(parts[3], "y", 1)]
    b_sums = [parts[4], shift(parts[5], "x", -1), shift(parts[6], "x", 2), shift(parts[7], "x", 1)]

    half = up_own.shape[1]
    over_rows = ((0,), (0,))
    down_theirs = mm(hidden_b[:, half:], grid_b, over_rows).astype(BF16)
    up_theirs = mm(rows_b, pgrad[:, half:], over_rows).astype(BF16)

    *q, up_theirs, down_theirs = sums(a_sums, b_sums, up_theirs, down_theirs)
    a_last = [q[0], shift(q[1], "x", -1), shift(q[2], "x", 2), shift(q[3], "x", 1)]
    b_last = [q[4], shift(q[5], "y", -1), shift(q[6], "y", 2), shift(q[7], "y", 1)]
    y_rows, dx_rows = call(rows_kernel, [out((SLOTS, d + 128))] * 2, "rows")(
        *a_last, *b_last, keep_f, keep_x, keep_g, keep_w, place_f, place_b, norm_gain
    )
    up_theirs, down_theirs = after((up_theirs, down_theirs), (y_rows,))
    up_theirs, down_theirs = shift(up_theirs, "core", 1), shift(down_theirs, "core", 1)
    grad_down = (mm(hidden_b[:, :half], grid_b, over_rows) + down_theirs.astype(F32)).astype(BF16)
    grad_up = (mm(rows_b, pgrad[:, :half], over_rows) + up_theirs.astype(F32)).astype(BF16)
    y_arrived = shift(y_rows, "pipe", 1)
    dx_arrived = shift(dx_rows, "pipe", -1)
    fwd_out, bwd_out = call(place_kernel, [out((tokens, d)), out((tokens, d))], "place", after=(6, 2))(
        base_f, y_arrived, base_b, dx_arrived, grad_up, grad_down
    )
    return (fwd_out[None], bwd_out[None], grad_up[None], grad_down[None])


def solution(mesh):
    chips = Mesh(mesh.devices.reshape(8, 4, 4, 2), ("pipe", "x", "y", "core"))
    expert = ("x", "y", "core")
    tokens = P("pipe", expert, None)
    return jax.shard_map(
        on_device,
        mesh=chips,
        in_specs=(tokens,) * 7 + (P("pipe", None), P("pipe", None, expert), P("pipe", expert, None)),
        out_specs=(tokens, tokens, P("pipe", None, expert), P("pipe", expert, None)),
        check_vma=False,
    )
```

```python
import functools

import jax
import jax.numpy as jnp
from jax import lax
from jax.experimental import pallas as pl
from jax.experimental.pallas import tpu as pltpu
from jax.sharding import Mesh, PartitionSpec as P

BF16 = jnp.bfloat16
F32 = jnp.float32
EPS = 1e-05
N_A = 13
N_B = 12
PAD = 16
SLOTS = 2 * PAD
GATH = 40
ROWS_A = 56
ROWS_B = 48


def shift(value, axis, by):
    count = lax.axis_size(axis)
    return lax.ppermute(value, axis, [(i, (i + by) % count) for i in range(count)])


def call(kernel, outs, name, vmem=20, after=None):
    count, unused = after or (0, 0)
    specs = {}
    if unused:
        whole, later = pl.BlockSpec(memory_space=pltpu.VMEM), pl.BlockSpec(memory_space=pl.ANY)
        specs = {"in_specs": [whole] * (count - unused) + [later] * unused}
    return pl.pallas_call(
        kernel,
        **specs,
        out_shape=outs,
        name=name,
        compiler_params=pltpu.CompilerParams(vmem_limit_bytes=vmem * 1000 * 1024),
    )


def out(shape, dtype=BF16):
    return jax.ShapeDtypeStruct(shape, dtype)


def iota(shape, dim):
    return lax.broadcasted_iota(jnp.int32, shape, dim)


def mm(a, b, dims=((1,), (0,)), precision=None):
    return lax.dot_general(a, b, (dims, ((), ())), preferred_element_type=F32, precision=precision)


def after(values, others):
    n = len(values)

    def nothing(*refs):
        pass

    hbm, anywhere = pl.BlockSpec(memory_space=pltpu.HBM), pl.BlockSpec(memory_space=pl.ANY)
    return pl.pallas_call(
        nothing,
        in_specs=[hbm] * n + [anywhere] * len(others),
        out_specs=[hbm] * n,
        out_shape=[pltpu.HBM(v.shape, v.dtype) for v in values],
        input_output_aliases={i: i for i in range(n)},
        name="after",
        compiler_params=pltpu.CompilerParams(vmem_limit_bytes=1 << 20),
    )(*values, *others)


def slots_of(ids):
    tokens = ids.shape[1]
    hit = jnp.where((ids[0:1] == 0) | (ids[1:2] == 0), 1.0, 0.0)
    hits = jnp.broadcast_to(hit, (SLOTS, tokens))
    before = jnp.where(iota((tokens, tokens), 0) < iota((tokens, tokens), 1), 1.0, 0.0)
    slot = mm(hits.astype(BF16), before.astype(BF16))
    place = jnp.where(slot > N_A - 0.5, slot + (PAD - N_A), slot)
    return jnp.where((hits > 0.5) & (place == iota((SLOTS, tokens), 0).astype(F32)), 1.0, 0.0)


def weights_of(ids, gates, chosen):
    gate = jnp.sum(jnp.where(ids == 0, gates, 0.0), axis=0, keepdims=True)
    return jnp.sum(chosen * gate, axis=1, keepdims=True)


def pack_kernel(
    xf, idf, gf, xb, idb, gb, grad, gain, send_a, send_b, keep_f, keep_x, keep_g, keep_w, place_f, place_b, ship_f, ship_b
):
    chosen_f = slots_of(idf[...])
    chosen_b = slots_of(idb[...])
    one_f = chosen_f.astype(BF16)
    one_b = chosen_b.astype(BF16)
    weight_f = weights_of(idf[...], gf[...], chosen_f)
    weight_b = weights_of(idb[...], gb[...], chosen_b)
    rows_f = mm(one_f, xf[...])
    rows_x = mm(one_b, xb[...])
    rows_g = mm(one_b, grad[...])

    def normal(rows):
        scale = lax.rsqrt(jnp.mean(rows * rows, axis=-1, keepdims=True) + EPS)
        return (rows * scale * gain[...]).astype(BF16)

    scaled = (rows_g * weight_b).astype(BF16)
    stacked = jnp.concatenate([normal(rows_f), normal(rows_x), scaled], axis=0)
    row, col = iota((2 * GATH, 3 * SLOTS), 0), iota((2 * GATH, 3 * SLOTS), 1)
    pick = jnp.zeros((2 * GATH, 3 * SLOTS), F32)
    for k in range(3):
        slot = col - SLOTS * k
        in_a = (slot >= 0) & (slot < N_A) & (row == slot + N_A * k)
        in_b = (slot >= PAD) & (slot < PAD + N_B) & (row == slot - PAD + N_B * k + GATH)
        pick = jnp.where(in_a | in_b, 1.0, pick)
    packed = mm(pick.astype(BF16), stacked)
    send_a[...] = packed[:GATH].astype(BF16)
    send_b[...] = packed[GATH:].astype(BF16)
    keep_f[...] = rows_f.astype(BF16)
    keep_x[...] = rows_x.astype(BF16)
    keep_g[...] = rows_g.astype(BF16)
    keep_w[...] = jnp.broadcast_to(weight_f, keep_w.shape)
    pad = jnp.zeros((SLOTS, 128 - xf.shape[0]), BF16)
    place_f[...] = jnp.concatenate([one_f, pad], axis=1)
    place_b[...] = jnp.concatenate([one_b, pad], axis=1)
    ship_f[...] = xf[...]
    ship_b[...] = grad[...]


def merge_rows(blocks, used, total):
    d = blocks[0].shape[1]
    stacked = jnp.concatenate([b[...] for b in blocks], axis=0)
    shape = (3 * total, 4 * GATH)
    row, col = iota(shape, 0), iota(shape, 1)
    pick = jnp.zeros(shape, F32)
    for k in range(3):
        for j in range(4):
            local = row - total * k - used * j
            good = (local >= 0) & (local < used) & (col == local + GATH * j + used * k)
            pick = jnp.where(good, 1.0, pick)
    moved = mm(pick.astype(BF16), stacked).astype(BF16)
    return [moved[total * k : total * (k + 1)] for k in range(3)], d


def merge_kernel(a0, a1, a2, a3, b0, b1, b2, b3, big_a, big_b):
    parts, d = merge_rows((a0, a1, a2, a3), N_A, ROWS_A)
    for k in range(3):
        big_a[:, k * d : (k + 1) * d] = parts[k]
    parts, d = merge_rows((b0, b1, b2, b3), N_B, ROWS_B)
    for k in range(3):
        big_b[:, k * d : (k + 1) * d] = parts[k]


def flip_kernel(own, other, across):
    half = own.shape[1]
    across[:half] = own[...].T
    across[half:] = other[...].T


def down_kernel(counts, hid, pg, dn, up, *refs):
    blocks = refs[len(refs) - len(counts) :]
    first = mm(hid[...], dn[...])
    second = mm(pg[...], up[...])
    start = 0
    for block in blocks:
        rows = block.shape[0] // 2
        block[:rows] = first[start : start + rows].astype(BF16)
        block[rows:] = second[start : start + rows].astype(BF16)
        start += rows


def down(hidden, pgrad, dn, up, counts, *after):
    rows, width = hidden.shape
    d = dn.shape[1]
    tile = 768
    whole = pl.BlockSpec((rows, width), lambda i: (0, 0))
    spec = pl.BlockSpec((width, tile), lambda i: (0, i))
    return pl.pallas_call(
        functools.partial(down_kernel, counts),
        grid=(d // tile,),
        in_specs=[whole, whole, spec, spec] + [pl.BlockSpec(memory_space=pl.ANY)] * len(after),
        out_specs=[pl.BlockSpec((2 * n, tile), lambda i: (0, i)) for n in counts],
        out_shape=[pltpu.HBM((2 * n, d), BF16) for n in counts],
        name="down",
        compiler_params=pltpu.CompilerParams(vmem_limit_bytes=16 * 1000 * 1024),
    )(hidden, pgrad, dn, up, *after)


def sum_rows(blocks, used, total):
    acc = blocks[0][...].astype(F32)
    for b in blocks[1:]:
        acc = acc + b[...].astype(F32)
    shape = (4 * SLOTS, 2 * total)
    row, col = iota(shape, 0), iota(shape, 1)
    pick = jnp.zeros(shape, F32)
    for j in range(4):
        for k in range(2):
            slot = row - SLOTS * j - PAD * k
            good = (slot >= 0) & (slot < used) & (col == slot + used * j + total * k)
            pick = jnp.where(good, 1.0, pick)
    moved = mm(pick.astype(BF16), acc.astype(BF16)).astype(BF16)
    return [moved[SLOTS * j : SLOTS * (j + 1)] for j in range(4)]


def sum_kernel(a0, a1, a2, a3, b0, b1, b2, b3, *refs):
    outs = refs[len(refs) // 2 - 4 :]
    parts = sum_rows((a0, a1, a2, a3), N_A, ROWS_A) + sum_rows((b0, b1, b2, b3), N_B, ROWS_B)
    for ref, part in zip(outs, parts):
        ref[...] = part


def sums(a_blocks, b_blocks, kept):
    d = a_blocks[0].shape[1]
    here, there = pl.BlockSpec(memory_space=pltpu.VMEM), pl.BlockSpec(memory_space=pltpu.HBM)
    return pl.pallas_call(
        sum_kernel,
        in_specs=[here] * 8 + [there] * len(kept),
        out_specs=[here] * 8 + [there] * len(kept),
        out_shape=[out((SLOTS, d))] * 8 + [pltpu.HBM(k.shape, k.dtype) for k in kept],
        input_output_aliases={8 + i: 8 + i for i in range(len(kept))},
        name="sums",
        compiler_params=pltpu.CompilerParams(vmem_limit_bytes=20 * 1000 * 1024),
    )(*a_blocks, *b_blocks, *kept)


def rows_kernel(
    a0, a1, a2, a3, b0, b1, b2, b3, keep_f, keep_x, keep_g, keep_w, place_f, place_b, gain, y_rows, dx_rows
):
    d = keep_f.shape[1]

    def total(refs):
        acc = refs[0][...].astype(F32)
        for r in refs[1:]:
            acc = acc + r[...].astype(F32)
        return acc.astype(BF16).astype(F32)

    part_a, part_b = total((a0, a1, a2, a3)), total((b0, b1, b2, b3))
    expert = jnp.concatenate([part_a[:PAD], part_b[:PAD]], axis=0)
    du = jnp.concatenate([part_a[PAD:], part_b[PAD:]], axis=0)
    y = keep_f[...].astype(F32) + keep_w[:, 0:1] * expert
    y_rows[:, :d] = y.astype(BF16)
    y_rows[:, d:] = place_f[...]
    x = keep_x[...].astype(F32)
    scale = lax.rsqrt(jnp.mean(x * x, axis=-1, keepdims=True) + EPS)
    h = du * gain[...]
    inner = jnp.mean(h * x, axis=-1, keepdims=True)
    dx = scale * h - x * (scale * scale * scale * inner)
    dx_rows[:, :d] = (keep_g[...].astype(F32) + dx).astype(BF16)
    dx_rows[:, d:] = place_b[...]


def place_kernel(base_f, y_rows, base_b, dx_rows, after_up, after_down, y_out, dx_out):
    tokens, d = base_f.shape
    ones = jnp.ones((SLOTS, 128), BF16)
    for base, rows, result in ((base_f, y_rows, y_out), (base_b, dx_rows, dx_out)):
        chosen = rows[:, d:]
        hit = mm(chosen, ones, ((0,), (0,)))[:tokens, 0:1]
        placed = mm(chosen, rows[:, :d], ((0,), (0,)))[:tokens]
        result[...] = jnp.where(hit > 0.5, placed, base[...].astype(F32)).astype(BF16)


def ring_gather(own, axis, first):
    ahead = shift(own, axis, 1)
    behind = shift(own, axis, -1)
    return [own, ahead, behind], [shift(ahead[:first], axis, 1), shift(behind[first:], axis, -1)]


def work(blocks, up, dn):
    rows = jnp.concatenate(blocks, axis=0)
    d = up.shape[1]
    rows_a, rows_b, grid_b = rows[:, :d], rows[:, d : 2 * d], rows[:, 2 * d :]
    pre_a = mm(rows_a, up, ((1,), (1,)))
    hidden_a = (pre_a * jax.nn.sigmoid(pre_a)).astype(BF16)
    pre_b = mm(rows_b, up, ((1,), (1,)))
    sigma = jax.nn.sigmoid(pre_b)
    hidden_b = (pre_b * sigma).astype(BF16)
    hidden_grad = mm(grid_b, dn, ((1,), (1,)))
    pgrad = (hidden_grad * sigma * (1.0 + pre_b * (1.0 - sigma))).astype(BF16)
    return hidden_a, (rows_b, grid_b, hidden_b, pgrad)


def on_device(
    fwd_in, fwd_ids, fwd_gate, bwd_in, bwd_ids, bwd_gate, bwd_grad, norm_gain, w_up, w_down
):
    tokens, d = fwd_in.shape[1:]
    send_a, send_b, keep_f, keep_x, keep_g, keep_w, place_f, place_b, base_f, base_b = call(
        pack_kernel,
        [pltpu.HBM((GATH, d), BF16)] * 2 + [out((SLOTS, d))] * 3 + [out((SLOTS, 128), F32)] + [out((SLOTS, 128))] * 2
        + [pltpu.HBM((tokens, d), BF16)] * 2,
        "pack",
        62,
    )(
        fwd_in[0],
        fwd_ids[0].T,
        fwd_gate[0].T,
        bwd_in[0],
        bwd_ids[0].T,
        bwd_gate[0].T,
        bwd_grad[0],
        norm_gain,
    )
    up_own, down_own = w_up[0], w_down[0]
    half = up_own.shape[1]
    up_other, down_other = shift(up_own, "core", 1), shift(down_own, "core", 1)
    send_a, send_b = after((send_a, send_b), (up_other, down_other))
    a_blocks = [send_a, shift(send_a, "x", 1), shift(send_a, "x", 2), shift(send_a, "x", -1)]
    b_blocks = [send_b, shift(send_b, "y", 1), shift(send_b, "y", 2), shift(send_b, "y", -1)]
    big_a, big_b = call(merge_kernel, [out((ROWS_A, 3 * d)), out((ROWS_B, 3 * d))], "merge")(
        *a_blocks, *b_blocks
    )
    [base_f] = after((base_f,), (big_a,))
    base_f = shift(base_f, "pipe", 1)
    [base_b] = after((base_b,), (base_f,))
    base_b = shift(base_b, "pipe", -1)
    dn = jnp.concatenate([down_own, down_other], axis=0)
    up = call(flip_kernel, out((2 * half, d)), "flip")(up_own, up_other)

    near_a, far_a = ring_gather(big_a, "y", 32)
    near_b, far_b = ring_gather(big_b, "x", 24)
    up, dn = after((up, dn), (far_b[0],))
    hidden_near, saved_near = work(near_a + near_b, up, dn)
    near = down(hidden_near, saved_near[3], dn, up, [ROWS_A] * 3 + [ROWS_B] * 3, base_f, base_b)
    hidden_far, saved_far = work(far_a + far_b, up, dn)
    far = down(hidden_far, saved_far[3], dn, up, [ROWS_A, ROWS_B])

    saved_far = (*saved_far[:2], *after(saved_far[2:], (far[0],)))

    a_sums = [near[0], shift(near[1], "y", -1), shift(far[0], "y", 2), shift(near[2], "y", 1)]
    b_sums = [near[3], shift(near[4], "x", -1), shift(far[1], "x", 2), shift(near[5], "x", 1)]

    over_rows = ((0,), (0,))

    def down_grad(saved, columns):
        return mm(saved[2][:, columns], saved[1], over_rows)

    def up_grad(saved, columns):
        return mm(saved[0], saved[3][:, columns], over_rows)

    theirs, mine = slice(half, None), slice(0, half)
    down_theirs = (down_grad(saved_near, theirs) + down_grad(saved_far, theirs)).astype(BF16)
    up_theirs = (up_grad(saved_near, theirs) + up_grad(saved_far, theirs)).astype(BF16)
    kept = (up_theirs, down_theirs, up_grad(saved_far, mine), down_grad(saved_far, mine))

    *q, up_theirs, down_theirs, up_mine, down_mine = sums(a_sums, b_sums, kept)
    a_last = [q[0], shift(q[1], "x", -1), shift(q[2], "x", 2), shift(q[3], "x", 1)]
    b_last = [q[4], shift(q[5], "y", -1), shift(q[6], "y", 2), shift(q[7], "y", 1)]
    y_rows, dx_rows = call(rows_kernel, [out((SLOTS, d + 128))] * 2, "rows")(
        *a_last, *b_last, keep_f, keep_x, keep_g, keep_w, place_f, place_b, norm_gain
    )
    up_theirs, down_theirs = after((up_theirs, down_theirs), (y_rows,))
    up_theirs, down_theirs = shift(up_theirs, "core", 1), shift(down_theirs, "core", 1)
    grad_down = (down_grad(saved_near, mine) + down_mine + down_theirs.astype(F32)).astype(BF16)
    grad_up = (up_grad(saved_near, mine) + up_mine + up_theirs.astype(F32)).astype(BF16)
    y_arrived = shift(y_rows, "pipe", 1)
    dx_arrived = shift(dx_rows, "pipe", -1)
    fwd_out, bwd_out = call(place_kernel, [out((tokens, d)), out((tokens, d))], "place", after=(6, 2))(
        base_f, y_arrived, base_b, dx_arrived, grad_up, grad_down
    )
    return (fwd_out[None], bwd_out[None], grad_up[None], grad_down[None])


def solution(mesh):
    chips = Mesh(mesh.devices.reshape(8, 4, 4, 2), ("pipe", "x", "y", "core"))
    expert = ("x", "y", "core")
    tokens = P("pipe", expert, None)
    return jax.shard_map(
        on_device,
        mesh=chips,
        in_specs=(tokens,) * 7 + (P("pipe", None), P("pipe", None, expert), P("pipe", expert, None)),
        out_specs=(tokens, tokens, P("pipe", None, expert), P("pipe", expert, None)),
        check_vma=False,
    )
```

```python
import functools

import jax
import jax.numpy as jnp
from jax import lax
from jax.experimental import pallas as pl
from jax.experimental.pallas import tpu as pltpu
from jax.sharding import Mesh, PartitionSpec as P

BF16 = jnp.bfloat16
F32 = jnp.float32
EPS = 1e-05
N_A = 13
N_B = 12
PAD = 16
SLOTS = 2 * PAD
GATH = 40
ROWS_A = 56
ROWS_B = 48


def shift(value, axis, by):
    count = lax.axis_size(axis)
    return lax.ppermute(value, axis, [(i, (i + by) % count) for i in range(count)])


def call(kernel, outs, name, vmem=20, after=None):
    count, unused = after or (0, 0)
    specs = {}
    if unused:
        whole, later = pl.BlockSpec(memory_space=pltpu.VMEM), pl.BlockSpec(memory_space=pl.ANY)
        specs = {"in_specs": [whole] * (count - unused) + [later] * unused}
    return pl.pallas_call(
        kernel,
        **specs,
        out_shape=outs,
        name=name,
        compiler_params=pltpu.CompilerParams(vmem_limit_bytes=vmem * 1000 * 1024),
    )


def out(shape, dtype=BF16):
    return jax.ShapeDtypeStruct(shape, dtype)


def iota(shape, dim):
    return lax.broadcasted_iota(jnp.int32, shape, dim)


def mm(a, b, dims=((1,), (0,)), precision=None):
    return lax.dot_general(a, b, (dims, ((), ())), preferred_element_type=F32, precision=precision)


def after(values, others, hbm=True):
    n = len(values)
    place = pltpu.HBM if hbm else pl.ANY
    shape = pltpu.HBM if hbm else jax.ShapeDtypeStruct

    def nothing(*refs):
        pass

    given, anywhere = pl.BlockSpec(memory_space=place), pl.BlockSpec(memory_space=pl.ANY)
    return pl.pallas_call(
        nothing,
        in_specs=[given] * n + [anywhere] * len(others),
        out_specs=[given] * n,
        out_shape=[shape(v.shape, v.dtype) for v in values],
        input_output_aliases={i: i for i in range(n)},
        name="after",
        compiler_params=pltpu.CompilerParams(vmem_limit_bytes=1 << 20),
    )(*values, *others)


def slots_of(ids):
    tokens = ids.shape[1]
    hit = jnp.where((ids[0:1] == 0) | (ids[1:2] == 0), 1.0, 0.0)
    hits = jnp.broadcast_to(hit, (SLOTS, tokens))
    before = jnp.where(iota((tokens, tokens), 0) < iota((tokens, tokens), 1), 1.0, 0.0)
    slot = mm(hits.astype(BF16), before.astype(BF16))
    place = jnp.where(slot > N_A - 0.5, slot + (PAD - N_A), slot)
    return jnp.where((hits > 0.5) & (place == iota((SLOTS, tokens), 0).astype(F32)), 1.0, 0.0)


def weights_of(ids, gates, chosen):
    gate = jnp.sum(jnp.where(ids == 0, gates, 0.0), axis=0, keepdims=True)
    return jnp.sum(chosen * gate, axis=1, keepdims=True)


def pack_kernel(
    xf, idf, gf, xb, idb, gb, grad, gain, send_a, send_b, keep_f, keep_x, keep_g, keep_w, place_f, place_b, ship_f, ship_b
):
    chosen_f = slots_of(idf[...])
    chosen_b = slots_of(idb[...])
    one_f = chosen_f.astype(BF16)
    one_b = chosen_b.astype(BF16)
    weight_f = weights_of(idf[...], gf[...], chosen_f)
    weight_b = weights_of(idb[...], gb[...], chosen_b)
    rows_f = mm(one_f, xf[...])
    rows_x = mm(one_b, xb[...])
    rows_g = mm(one_b, grad[...])

    def normal(rows):
        scale = lax.rsqrt(jnp.mean(rows * rows, axis=-1, keepdims=True) + EPS)
        return (rows * scale * gain[...]).astype(BF16)

    scaled = (rows_g * weight_b).astype(BF16)
    stacked = jnp.concatenate([normal(rows_f), normal(rows_x), scaled], axis=0)
    row, col = iota((2 * GATH, 3 * SLOTS), 0), iota((2 * GATH, 3 * SLOTS), 1)
    pick = jnp.zeros((2 * GATH, 3 * SLOTS), F32)
    for k in range(3):
        slot = col - SLOTS * k
        in_a = (slot >= 0) & (slot < N_A) & (row == slot + N_A * k)
        in_b = (slot >= PAD) & (slot < PAD + N_B) & (row == slot - PAD + N_B * k + GATH)
        pick = jnp.where(in_a | in_b, 1.0, pick)
    packed = mm(pick.astype(BF16), stacked)
    send_a[...] = packed[:GATH].astype(BF16)
    send_b[...] = packed[GATH:].astype(BF16)
    keep_f[...] = rows_f.astype(BF16)
    keep_x[...] = rows_x.astype(BF16)
    keep_g[...] = rows_g.astype(BF16)
    keep_w[...] = jnp.broadcast_to(weight_f, keep_w.shape)
    pad = jnp.zeros((SLOTS, 128 - xf.shape[0]), BF16)
    place_f[...] = jnp.concatenate([one_f, pad], axis=1)
    place_b[...] = jnp.concatenate([one_b, pad], axis=1)
    ship_f[...] = xf[...]
    ship_b[...] = grad[...]


def merge_rows(blocks, used, total):
    d = blocks[0].shape[1]
    stacked = jnp.concatenate([b[...] for b in blocks], axis=0)
    shape = (3 * total, 4 * GATH)
    row, col = iota(shape, 0), iota(shape, 1)
    pick = jnp.zeros(shape, F32)
    for k in range(3):
        for j in range(4):
            local = row - total * k - used * j
            good = (local >= 0) & (local < used) & (col == local + GATH * j + used * k)
            pick = jnp.where(good, 1.0, pick)
    moved = mm(pick.astype(BF16), stacked).astype(BF16)
    return [moved[total * k : total * (k + 1)] for k in range(3)], d


def merge_kernel(a0, a1, a2, a3, b0, b1, b2, b3, big_a, big_b):
    parts, d = merge_rows((a0, a1, a2, a3), N_A, ROWS_A)
    for k in range(3):
        big_a[:, k * d : (k + 1) * d] = parts[k]
    parts, d = merge_rows((b0, b1, b2, b3), N_B, ROWS_B)
    for k in range(3):
        big_b[:, k * d : (k + 1) * d] = parts[k]


def flip_kernel(up_own, up_other, down_own, down_other, after_merge, up, dn):
    half = up_own.shape[1]
    up[:half] = up_own[...].T
    up[half:] = up_other[...].T
    dn[:half] = down_own[...]
    dn[half:] = down_other[...]


def down_kernel(counts, hid, pg, dn, up, *refs):
    blocks = refs[len(refs) - len(counts) :]
    first = mm(hid[...], dn[...])
    second = mm(pg[...], up[...])
    start = 0
    for block in blocks:
        rows = block.shape[0] // 2
        block[:rows] = first[start : start + rows].astype(BF16)
        block[rows:] = second[start : start + rows].astype(BF16)
        start += rows


def down(hidden, pgrad, dn, up, counts, *after):
    rows, width = hidden.shape
    d = dn.shape[1]
    tile = 768
    whole = pl.BlockSpec((rows, width), lambda i: (0, 0))
    spec = pl.BlockSpec((width, tile), lambda i: (0, i))
    return pl.pallas_call(
        functools.partial(down_kernel, counts),
        grid=(d // tile,),
        in_specs=[whole, whole, spec, spec] + [pl.BlockSpec(memory_space=pl.ANY)] * len(after),
        out_specs=[pl.BlockSpec((2 * n, tile), lambda i: (0, i)) for n in counts],
        out_shape=[pltpu.HBM((2 * n, d), BF16) for n in counts],
        name="down",
        compiler_params=pltpu.CompilerParams(vmem_limit_bytes=16 * 1000 * 1024),
    )(hidden, pgrad, dn, up, *after)


def sum_rows(blocks, used, total):
    acc = blocks[0][...].astype(F32)
    for b in blocks[1:]:
        acc = acc + b[...].astype(F32)
    shape = (4 * SLOTS, 2 * total)
    row, col = iota(shape, 0), iota(shape, 1)
    pick = jnp.zeros(shape, F32)
    for j in range(4):
        for k in range(2):
            slot = row - SLOTS * j - PAD * k
            good = (slot >= 0) & (slot < used) & (col == slot + used * j + total * k)
            pick = jnp.where(good, 1.0, pick)
    moved = mm(pick.astype(BF16), acc.astype(BF16)).astype(BF16)
    return [moved[SLOTS * j : SLOTS * (j + 1)] for j in range(4)]


def sum_kernel(a0, a1, a2, a3, b0, b1, b2, b3, *outs):
    parts = sum_rows((a0, a1, a2, a3), N_A, ROWS_A) + sum_rows((b0, b1, b2, b3), N_B, ROWS_B)
    for ref, part in zip(outs, parts):
        ref[...] = part


def rows_kernel(
    a0, a1, a2, a3, b0, b1, b2, b3, keep_f, keep_x, keep_g, keep_w, place_f, place_b, gain, after_up, after_down,
    y_rows, dx_rows
):
    d = keep_f.shape[1]

    def total(refs):
        acc = refs[0][...].astype(F32)
        for r in refs[1:]:
            acc = acc + r[...].astype(F32)
        return acc.astype(BF16).astype(F32)

    part_a, part_b = total((a0, a1, a2, a3)), total((b0, b1, b2, b3))
    expert = jnp.concatenate([part_a[:PAD], part_b[:PAD]], axis=0)
    du = jnp.concatenate([part_a[PAD:], part_b[PAD:]], axis=0)
    y = keep_f[...].astype(F32) + keep_w[:, 0:1] * expert
    y_rows[:, :d] = y.astype(BF16)
    y_rows[:, d:] = place_f[...]
    x = keep_x[...].astype(F32)
    scale = lax.rsqrt(jnp.mean(x * x, axis=-1, keepdims=True) + EPS)
    h = du * gain[...]
    inner = jnp.mean(h * x, axis=-1, keepdims=True)
    dx = scale * h - x * (scale * scale * scale * inner)
    dx_rows[:, :d] = (keep_g[...].astype(F32) + dx).astype(BF16)
    dx_rows[:, d:] = place_b[...]


def place_kernel(base_f, y_rows, base_b, dx_rows, y_out, dx_out):
    tokens, d = base_f.shape
    ones = jnp.ones((SLOTS, 128), BF16)
    for base, rows, result in ((base_f, y_rows, y_out), (base_b, dx_rows, dx_out)):
        chosen = rows[:, d:]
        hit = mm(chosen, ones, ((0,), (0,)))[:tokens, 0:1]
        placed = mm(chosen, rows[:, :d], ((0,), (0,)))[:tokens]
        result[...] = jnp.where(hit > 0.5, placed, base[...].astype(F32)).astype(BF16)


def ring_gather(own, axis, first):
    ahead = shift(own, axis, 1)
    behind = shift(own, axis, -1)
    return [own, ahead, behind], [shift(ahead[:first], axis, 1), shift(behind[first:], axis, -1)]


def work(blocks, up, dn):
    rows = jnp.concatenate(blocks, axis=0)
    d = up.shape[1]
    rows_a, rows_b, grid_b = rows[:, :d], rows[:, d : 2 * d], rows[:, 2 * d :]
    pre_a = mm(rows_a, up, ((1,), (1,)))
    hidden_a = (pre_a * jax.nn.sigmoid(pre_a)).astype(BF16)
    pre_b = mm(rows_b, up, ((1,), (1,)))
    sigma = jax.nn.sigmoid(pre_b)
    hidden_b = (pre_b * sigma).astype(BF16)
    hidden_grad = mm(grid_b, dn, ((1,), (1,)))
    pgrad = (hidden_grad * sigma * (1.0 + pre_b * (1.0 - sigma))).astype(BF16)
    return hidden_a, (rows_b, grid_b, hidden_b, pgrad)


def on_device(
    fwd_in, fwd_ids, fwd_gate, bwd_in, bwd_ids, bwd_gate, bwd_grad, norm_gain, w_up, w_down
):
    tokens, d = fwd_in.shape[1:]
    send_a, send_b, keep_f, keep_x, keep_g, keep_w, place_f, place_b, base_f, base_b = call(
        pack_kernel,
        [pltpu.HBM((GATH, d), BF16)] * 2 + [out((SLOTS, d))] * 3 + [out((SLOTS, 128), F32)] + [out((SLOTS, 128))] * 2
        + [pltpu.HBM((tokens, d), BF16)] * 2,
        "pack",
        62,
    )(
        fwd_in[0],
        fwd_ids[0].T,
        fwd_gate[0].T,
        bwd_in[0],
        bwd_ids[0].T,
        bwd_gate[0].T,
        bwd_grad[0],
        norm_gain,
    )
    up_own, down_own = w_up[0], w_down[0]
    half = up_own.shape[1]
    up_other, down_other = shift(up_own, "core", 1), shift(down_own, "core", 1)
    send_a, send_b = after((send_a, send_b), (up_other, down_other))
    a_blocks = [send_a, shift(send_a, "x", 1), shift(send_a, "x", 2), shift(send_a, "x", -1)]
    b_blocks = [send_b, shift(send_b, "y", 1), shift(send_b, "y", 2), shift(send_b, "y", -1)]
    big_a, big_b = call(merge_kernel, [out((ROWS_A, 3 * d)), out((ROWS_B, 3 * d))], "merge")(
        *a_blocks, *b_blocks
    )
    [base_f] = after((base_f,), (big_a,))
    base_f = shift(base_f, "pipe", 1)
    [base_b] = after((base_b,), (base_f,))
    base_b = shift(base_b, "pipe", -1)
    up, dn = call(flip_kernel, [out((2 * half, d))] * 2, "flip", after=(5, 1))(
        up_own, up_other, down_own, down_other, big_a
    )

    near_a, far_a = ring_gather(big_a, "y", 32)
    near_b, far_b = ring_gather(big_b, "x", 24)
    up, dn = after((up, dn), (far_b[0],), hbm=False)
    hidden_near, saved_near = work(near_a + near_b, up, dn)
    near = down(hidden_near, saved_near[3], dn, up, [ROWS_A] * 3 + [ROWS_B] * 3, base_f, base_b)
    hidden_far, saved_far = work(far_a + far_b, up, dn)
    far = down(hidden_far, saved_far[3], dn, up, [ROWS_A, ROWS_B])

    a_sums = [near[0], shift(near[1], "y", -1), shift(far[0], "y", 2), shift(near[2], "y", 1)]
    b_sums = [near[3], shift(near[4], "x", -1), shift(far[1], "x", 2), shift(near[5], "x", 1)]

    saved_far = (*saved_far[:2], *after(saved_far[2:], (b_sums[1], far[0])))
    over_rows = ((0,), (0,))

    def down_grad(saved, columns):
        return mm(saved[2][:, columns], saved[1], over_rows)

    def up_grad(saved, columns):
        return mm(saved[0], saved[3][:, columns], over_rows)

    theirs, mine = slice(half, None), slice(0, half)
    down_theirs = (down_grad(saved_near, theirs) + down_grad(saved_far, theirs)).astype(BF16)
    up_theirs = (up_grad(saved_near, theirs) + up_grad(saved_far, theirs)).astype(BF16)
    up_mine, down_mine = up_grad(saved_far, mine), down_grad(saved_far, mine)
    up_theirs, down_theirs, up_mine, down_mine = after(
        (up_theirs, down_theirs, up_mine, down_mine), (*a_sums[1:], *b_sums[1:])
    )
    q = call(sum_kernel, [out((SLOTS, d))] * 8, "sums")(*a_sums, *b_sums)
    up_theirs, down_theirs = after((up_theirs, down_theirs), (q[0],))
    up_theirs, down_theirs = shift(up_theirs, "core", 1), shift(down_theirs, "core", 1)
    grad_down = (down_grad(saved_near, mine) + down_mine + down_theirs.astype(F32)).astype(BF16)
    grad_up = (up_grad(saved_near, mine) + up_mine + up_theirs.astype(F32)).astype(BF16)

    a_last = [q[0], shift(q[1], "x", -1), shift(q[2], "x", 2), shift(q[3], "x", 1)]
    b_last = [q[4], shift(q[5], "y", -1), shift(q[6], "y", 2), shift(q[7], "y", 1)]
    y_rows, dx_rows = call(rows_kernel, [out((SLOTS, d + 128))] * 2, "rows", after=(17, 2))(
        *a_last, *b_last, keep_f, keep_x, keep_g, keep_w, place_f, place_b, norm_gain, grad_up, grad_down
    )
    y_arrived = shift(y_rows, "pipe", 1)
    dx_arrived = shift(dx_rows, "pipe", -1)
    fwd_out, bwd_out = call(place_kernel, [out((tokens, d)), out((tokens, d))], "place")(
        base_f, y_arrived, base_b, dx_arrived
    )
    return (fwd_out[None], bwd_out[None], grad_up[None], grad_down[None])


def solution(mesh):
    chips = Mesh(mesh.devices.reshape(8, 4, 4, 2), ("pipe", "x", "y", "core"))
    expert = ("x", "y", "core")
    tokens = P("pipe", expert, None)
    return jax.shard_map(
        on_device,
        mesh=chips,
        in_specs=(tokens,) * 7 + (P("pipe", None), P("pipe", None, expert), P("pipe", expert, None)),
        out_specs=(tokens, tokens, P("pipe", None, expert), P("pipe", expert, None)),
        check_vma=False,
    )
```

```python
import functools

import jax
import jax.numpy as jnp
from jax import lax
from jax.experimental import pallas as pl
from jax.experimental.pallas import tpu as pltpu
from jax.sharding import Mesh, PartitionSpec as P

BF16 = jnp.bfloat16
F32 = jnp.float32
EPS = 1e-05
N_A = 13
N_B = 12
PAD = 16
SLOTS = 2 * PAD
GATH = 40
ROWS_A = 56
ROWS_B = 48


def shift(value, axis, by):
    count = lax.axis_size(axis)
    return lax.ppermute(value, axis, [(i, (i + by) % count) for i in range(count)])


def call(kernel, outs, name, vmem=20, after=None):
    count, unused = after or (0, 0)
    specs = {}
    if unused:
        whole, later = pl.BlockSpec(memory_space=pltpu.VMEM), pl.BlockSpec(memory_space=pl.ANY)
        specs = {"in_specs": [whole] * (count - unused) + [later] * unused}
    return pl.pallas_call(
        kernel,
        **specs,
        out_shape=outs,
        name=name,
        compiler_params=pltpu.CompilerParams(vmem_limit_bytes=vmem * 1000 * 1024),
    )


def out(shape, dtype=BF16):
    return jax.ShapeDtypeStruct(shape, dtype)


def iota(shape, dim):
    return lax.broadcasted_iota(jnp.int32, shape, dim)


def mm(a, b, dims=((1,), (0,)), precision=None):
    return lax.dot_general(a, b, (dims, ((), ())), preferred_element_type=F32, precision=precision)


def after(values, others, hbm=True):
    n = len(values)
    place = pltpu.HBM if hbm else pl.ANY
    shape = pltpu.HBM if hbm else jax.ShapeDtypeStruct

    def nothing(*refs):
        pass

    given, anywhere = pl.BlockSpec(memory_space=place), pl.BlockSpec(memory_space=pl.ANY)
    return pl.pallas_call(
        nothing,
        in_specs=[given] * n + [anywhere] * len(others),
        out_specs=[given] * n,
        out_shape=[shape(v.shape, v.dtype) for v in values],
        input_output_aliases={i: i for i in range(n)},
        name="after",
        compiler_params=pltpu.CompilerParams(vmem_limit_bytes=1 << 20),
    )(*values, *others)


def slots_of(ids):
    tokens = ids.shape[1]
    hit = jnp.where((ids[0:1] == 0) | (ids[1:2] == 0), 1.0, 0.0)
    hits = jnp.broadcast_to(hit, (SLOTS, tokens))
    before = jnp.where(iota((tokens, tokens), 0) < iota((tokens, tokens), 1), 1.0, 0.0)
    slot = mm(hits.astype(BF16), before.astype(BF16))
    place = jnp.where(slot > N_A - 0.5, slot + (PAD - N_A), slot)
    return jnp.where((hits > 0.5) & (place == iota((SLOTS, tokens), 0).astype(F32)), 1.0, 0.0)


def weights_of(ids, gates, chosen):
    gate = jnp.sum(jnp.where(ids == 0, gates, 0.0), axis=0, keepdims=True)
    return jnp.sum(chosen * gate, axis=1, keepdims=True)


def pack_kernel(
    xf, idf, gf, xb, idb, gb, grad, gain, send_a, send_b, keep_f, keep_x, keep_g, keep_w, place_f, place_b, ship_f, ship_b,
    own_a, own_b
):
    chosen_f = slots_of(idf[...])
    chosen_b = slots_of(idb[...])
    one_f = chosen_f.astype(BF16)
    one_b = chosen_b.astype(BF16)
    weight_f = weights_of(idf[...], gf[...], chosen_f)
    weight_b = weights_of(idb[...], gb[...], chosen_b)
    rows_f = mm(one_f, xf[...])
    rows_x = mm(one_b, xb[...])
    rows_g = mm(one_b, grad[...])

    def normal(rows):
        scale = lax.rsqrt(jnp.mean(rows * rows, axis=-1, keepdims=True) + EPS)
        return (rows * scale * gain[...]).astype(BF16)

    scaled = (rows_g * weight_b).astype(BF16)
    stacked = jnp.concatenate([normal(rows_f), normal(rows_x), scaled], axis=0)
    row, col = iota((2 * GATH, 3 * SLOTS), 0), iota((2 * GATH, 3 * SLOTS), 1)
    pick = jnp.zeros((2 * GATH, 3 * SLOTS), F32)
    for k in range(3):
        slot = col - SLOTS * k
        in_a = (slot >= 0) & (slot < N_A) & (row == slot + N_A * k)
        in_b = (slot >= PAD) & (slot < PAD + N_B) & (row == slot - PAD + N_B * k + GATH)
        pick = jnp.where(in_a | in_b, 1.0, pick)
    packed = mm(pick.astype(BF16), stacked)
    send_a[...] = packed[:GATH].astype(BF16)
    send_b[...] = packed[GATH:].astype(BF16)
    own_a[...] = packed[:GATH].astype(BF16)
    own_b[...] = packed[GATH:].astype(BF16)
    keep_f[...] = rows_f.astype(BF16)
    keep_x[...] = rows_x.astype(BF16)
    keep_g[...] = rows_g.astype(BF16)
    keep_w[...] = jnp.broadcast_to(weight_f, keep_w.shape)
    pad = jnp.zeros((SLOTS, 128 - xf.shape[0]), BF16)
    place_f[...] = jnp.concatenate([one_f, pad], axis=1)
    place_b[...] = jnp.concatenate([one_b, pad], axis=1)
    ship_f[...] = xf[...]
    ship_b[...] = grad[...]


def merge_rows(blocks, used, total):
    d = blocks[0].shape[1]
    stacked = jnp.concatenate([b[...] for b in blocks], axis=0)
    shape = (3 * total, 4 * GATH)
    row, col = iota(shape, 0), iota(shape, 1)
    pick = jnp.zeros(shape, F32)
    for k in range(3):
        for j in range(4):
            local = row - total * k - used * j
            good = (local >= 0) & (local < used) & (col == local + GATH * j + used * k)
            pick = jnp.where(good, 1.0, pick)
    moved = mm(pick.astype(BF16), stacked).astype(BF16)
    return [moved[total * k : total * (k + 1)] for k in range(3)], d


def merge_kernel(a0, a1, a2, a3, b0, b1, b2, b3, big_a, big_b):
    parts, d = merge_rows((a0, a1, a2, a3), N_A, ROWS_A)
    for k in range(3):
        big_a[:, k * d : (k + 1) * d] = parts[k]
    parts, d = merge_rows((b0, b1, b2, b3), N_B, ROWS_B)
    for k in range(3):
        big_b[:, k * d : (k + 1) * d] = parts[k]


def flip_kernel(up_own, up_other, down_own, down_other, after_merge, up, dn):
    half = up_own.shape[1]
    up[:half] = up_own[...].T
    up[half:] = up_other[...].T
    dn[:half] = down_own[...]
    dn[half:] = down_other[...]


def down_kernel(counts, hid, pg, dn, up, *refs):
    blocks = refs[len(refs) - len(counts) :]
    first = mm(hid[...], dn[...])
    second = mm(pg[...], up[...])
    start = 0
    for block in blocks:
        rows = block.shape[0] // 2
        block[:rows] = first[start : start + rows].astype(BF16)
        block[rows:] = second[start : start + rows].astype(BF16)
        start += rows


def down(hidden, pgrad, dn, up, counts, *after):
    rows, width = hidden.shape
    d = dn.shape[1]
    tile = 768
    whole = pl.BlockSpec((rows, width), lambda i: (0, 0))
    spec = pl.BlockSpec((width, tile), lambda i: (0, i))
    return pl.pallas_call(
        functools.partial(down_kernel, counts),
        grid=(d // tile,),
        in_specs=[whole, whole, spec, spec] + [pl.BlockSpec(memory_space=pl.ANY)] * len(after),
        out_specs=[pl.BlockSpec((2 * n, tile), lambda i: (0, i)) for n in counts],
        out_shape=[pltpu.HBM((2 * n, d), BF16) for n in counts],
        name="down",
        compiler_params=pltpu.CompilerParams(vmem_limit_bytes=16 * 1000 * 1024),
    )(hidden, pgrad, dn, up, *after)


def sum_rows(blocks, used, total):
    acc = blocks[0][...].astype(F32)
    for b in blocks[1:]:
        acc = acc + b[...].astype(F32)
    shape = (4 * SLOTS, 2 * total)
    row, col = iota(shape, 0), iota(shape, 1)
    pick = jnp.zeros(shape, F32)
    for j in range(4):
        for k in range(2):
            slot = row - SLOTS * j - PAD * k
            good = (slot >= 0) & (slot < used) & (col == slot + used * j + total * k)
            pick = jnp.where(good, 1.0, pick)
    moved = mm(pick.astype(BF16), acc.astype(BF16)).astype(BF16)
    return [moved[SLOTS * j : SLOTS * (j + 1)] for j in range(4)]


def sum_kernel(a0, a1, a2, a3, b0, b1, b2, b3, *outs):
    parts = sum_rows((a0, a1, a2, a3), N_A, ROWS_A) + sum_rows((b0, b1, b2, b3), N_B, ROWS_B)
    for ref, part in zip(outs, parts):
        ref[...] = part


def rows_kernel(
    a0, a1, a2, a3, b0, b1, b2, b3, keep_f, keep_x, keep_g, keep_w, place_f, place_b, gain, y_rows, dx_rows
):
    d = keep_f.shape[1]

    def total(refs):
        acc = refs[0][...].astype(F32)
        for r in refs[1:]:
            acc = acc + r[...].astype(F32)
        return acc.astype(BF16).astype(F32)

    part_a, part_b = total((a0, a1, a2, a3)), total((b0, b1, b2, b3))
    expert = jnp.concatenate([part_a[:PAD], part_b[:PAD]], axis=0)
    du = jnp.concatenate([part_a[PAD:], part_b[PAD:]], axis=0)
    y = keep_f[...].astype(F32) + keep_w[:, 0:1] * expert
    y_rows[:, :d] = y.astype(BF16)
    y_rows[:, d:] = place_f[...]
    x = keep_x[...].astype(F32)
    scale = lax.rsqrt(jnp.mean(x * x, axis=-1, keepdims=True) + EPS)
    h = du * gain[...]
    inner = jnp.mean(h * x, axis=-1, keepdims=True)
    dx = scale * h - x * (scale * scale * scale * inner)
    dx_rows[:, :d] = (keep_g[...].astype(F32) + dx).astype(BF16)
    dx_rows[:, d:] = place_b[...]


def place_kernel(base_f, y_rows, base_b, dx_rows, after_up, after_down, y_out, dx_out):
    tokens, d = base_f.shape
    ones = jnp.ones((SLOTS, 128), BF16)
    for base, rows, result in ((base_f, y_rows, y_out), (base_b, dx_rows, dx_out)):
        chosen = rows[:, d:]
        hit = mm(chosen, ones, ((0,), (0,)))[:tokens, 0:1]
        placed = mm(chosen, rows[:, :d], ((0,), (0,)))[:tokens]
        result[...] = jnp.where(hit > 0.5, placed, base[...].astype(F32)).astype(BF16)


def both(own_a, a, a_axis, own_b, b, b_axis, sign, wait=None):
    a1, a3 = shift(a[0], a_axis, sign), shift(a[2], a_axis, -sign)
    b1, b3 = shift(b[0], b_axis, sign), shift(b[2], b_axis, -sign)
    a2, b2 = a[1], b[1]
    if wait == "both":
        a2, b2 = after((a2, b2), (a1, b1))
    elif wait == "b":
        [b2] = after((b2,), (b1,))
    a2, b2 = shift(a2, a_axis, 2), shift(b2, b_axis, 2)
    return [own_a, a1, a2, a3], [own_b, b1, b2, b3]


def ring_gather(own, axis, first):
    ahead = shift(own, axis, 1)
    behind = shift(own, axis, -1)
    return [own, ahead, behind], [shift(ahead[:first], axis, 1), shift(behind[first:], axis, -1)]


def work(blocks, up, dn):
    rows = jnp.concatenate(blocks, axis=0)
    d = up.shape[1]
    rows_a, rows_b, grid_b = rows[:, :d], rows[:, d : 2 * d], rows[:, 2 * d :]
    pre_a = mm(rows_a, up, ((1,), (1,)))
    hidden_a = (pre_a * jax.nn.sigmoid(pre_a)).astype(BF16)
    pre_b = mm(rows_b, up, ((1,), (1,)))
    sigma = jax.nn.sigmoid(pre_b)
    hidden_b = (pre_b * sigma).astype(BF16)
    hidden_grad = mm(grid_b, dn, ((1,), (1,)))
    pgrad = (hidden_grad * sigma * (1.0 + pre_b * (1.0 - sigma))).astype(BF16)
    return hidden_a, (rows_b, grid_b, hidden_b, pgrad)


def on_device(
    fwd_in, fwd_ids, fwd_gate, bwd_in, bwd_ids, bwd_gate, bwd_grad, norm_gain, w_up, w_down
):
    tokens, d = fwd_in.shape[1:]
    send_a, send_b, keep_f, keep_x, keep_g, keep_w, place_f, place_b, base_f, base_b, own_a, own_b = call(
        pack_kernel,
        [pltpu.HBM((GATH, d), BF16)] * 2 + [out((SLOTS, d))] * 3 + [out((SLOTS, 128), F32)] + [out((SLOTS, 128))] * 2
        + [pltpu.HBM((tokens, d), BF16)] * 2 + [out((GATH, d))] * 2,
        "pack",
        62,
    )(
        fwd_in[0],
        fwd_ids[0].T,
        fwd_gate[0].T,
        bwd_in[0],
        bwd_ids[0].T,
        bwd_gate[0].T,
        bwd_grad[0],
        norm_gain,
    )
    up_own, down_own = w_up[0], w_down[0]
    half = up_own.shape[1]
    up_other, down_other = shift(up_own, "core", 1), shift(down_own, "core", 1)
    send_a, send_b = after((send_a, send_b), (up_other, down_other))
    a_blocks, b_blocks = both(own_a, [send_a] * 3, "x", own_b, [send_b] * 3, "y", 1, "both")
    big_a, big_b = call(merge_kernel, [out((ROWS_A, 3 * d)), out((ROWS_B, 3 * d))], "merge")(
        *a_blocks, *b_blocks
    )
    [base_f] = after((base_f,), (big_a,))
    base_f = shift(base_f, "pipe", 1)
    [base_b] = after((base_b,), (base_f,))
    base_b = shift(base_b, "pipe", -1)
    up, dn = call(flip_kernel, [out((2 * half, d))] * 2, "flip", after=(5, 1))(
        up_own, up_other, down_own, down_other, big_a
    )

    near_a, far_a = ring_gather(big_a, "y", 32)
    near_b, far_b = ring_gather(big_b, "x", 24)
    up, dn = after((up, dn), (far_b[0],), hbm=False)
    hidden_near, saved_near = work(near_a + near_b, up, dn)
    near = down(hidden_near, saved_near[3], dn, up, [ROWS_A] * 3 + [ROWS_B] * 3, base_f, base_b)
    hidden_far, saved_far = work(far_a + far_b, up, dn)
    far = down(hidden_far, saved_far[3], dn, up, [ROWS_A, ROWS_B])

    a_sums, b_sums = both(
        near[0], (near[1], far[0], near[2]), "y", near[3], (near[4], far[1], near[5]), "x", -1, "b"
    )
    saved_far = (*saved_far[:2], *after(saved_far[2:], (b_sums[1], far[0])))
    over_rows = ((0,), (0,))

    def down_grad(saved, columns):
        return mm(saved[2][:, columns], saved[1], over_rows)

    def up_grad(saved, columns):
        return mm(saved[0], saved[3][:, columns], over_rows)

    theirs, mine = slice(half, None), slice(0, half)
    down_theirs = (down_grad(saved_near, theirs) + down_grad(saved_far, theirs)).astype(BF16)
    up_theirs = (up_grad(saved_near, theirs) + up_grad(saved_far, theirs)).astype(BF16)
    up_mine, down_mine = up_grad(saved_far, mine), down_grad(saved_far, mine)
    up_theirs, down_theirs, up_mine, down_mine = after(
        (up_theirs, down_theirs, up_mine, down_mine), (*a_sums[1:], *b_sums[1:])
    )
    q = call(sum_kernel, [out((SLOTS, d))] * 8, "sums")(*a_sums, *b_sums)
    a_last, b_last = both(q[0], q[1:4], "x", q[4], q[5:8], "y", -1)
    y_rows, dx_rows = call(rows_kernel, [out((SLOTS, d + 128))] * 2, "rows")(
        *a_last, *b_last, keep_f, keep_x, keep_g, keep_w, place_f, place_b, norm_gain
    )
    up_theirs, down_theirs = after((up_theirs, down_theirs), (y_rows,))
    up_theirs, down_theirs = shift(up_theirs, "core", 1), shift(down_theirs, "core", 1)
    grad_down = (down_grad(saved_near, mine) + down_mine + down_theirs.astype(F32)).astype(BF16)
    grad_up = (up_grad(saved_near, mine) + up_mine + up_theirs.astype(F32)).astype(BF16)
    y_arrived = shift(y_rows, "pipe", 1)
    dx_arrived = shift(dx_rows, "pipe", -1)
    fwd_out, bwd_out = call(place_kernel, [out((tokens, d)), out((tokens, d))], "place", after=(6, 2))(
        base_f, y_arrived, base_b, dx_arrived, grad_up, grad_down
    )
    return (fwd_out[None], bwd_out[None], grad_up[None], grad_down[None])


def solution(mesh):
    chips = Mesh(mesh.devices.reshape(8, 4, 4, 2), ("pipe", "x", "y", "core"))
    expert = ("x", "y", "core")
    tokens = P("pipe", expert, None)
    return jax.shard_map(
        on_device,
        mesh=chips,
        in_specs=(tokens,) * 7 + (P("pipe", None), P("pipe", None, expert), P("pipe", expert, None)),
        out_specs=(tokens, tokens, P("pipe", None, expert), P("pipe", expert, None)),
        check_vma=False,
    )
```

```python
import functools

import jax
import jax.numpy as jnp
from jax import lax
from jax.experimental import pallas as pl
from jax.experimental.pallas import tpu as pltpu
from jax.sharding import Mesh, PartitionSpec as P

BF16 = jnp.bfloat16
F32 = jnp.float32
EPS = 1e-05
N_A = 13
N_B = 12
PAD = 16
SLOTS = 2 * PAD
GATH = 40
ROWS_A = 56
ROWS_B = 48


def shift(value, axis, by):
    count = lax.axis_size(axis)
    return lax.ppermute(value, axis, [(i, (i + by) % count) for i in range(count)])


def call(kernel, outs, name, vmem=20, after=None):
    count, unused = after or (0, 0)
    specs = {}
    if count:
        whole, later = pl.BlockSpec(memory_space=pltpu.VMEM), pl.BlockSpec(memory_space=pl.ANY)
        specs = {"in_specs": [whole] * (count - unused) + [later] * unused}
    return pl.pallas_call(
        kernel,
        **specs,
        out_shape=outs,
        name=name,
        compiler_params=pltpu.CompilerParams(vmem_limit_bytes=vmem * 1000 * 1024),
    )


def out(shape, dtype=BF16):
    return jax.ShapeDtypeStruct(shape, dtype)


def iota(shape, dim):
    return lax.broadcasted_iota(jnp.int32, shape, dim)


def mm(a, b, dims=((1,), (0,)), precision=None):
    return lax.dot_general(a, b, (dims, ((), ())), preferred_element_type=F32, precision=precision)


def after(values, others, hbm=True):
    n = len(values)
    place = pltpu.HBM if hbm else pl.ANY
    shape = pltpu.HBM if hbm else jax.ShapeDtypeStruct

    def nothing(*refs):
        pass

    given, anywhere = pl.BlockSpec(memory_space=place), pl.BlockSpec(memory_space=pl.ANY)
    return pl.pallas_call(
        nothing,
        in_specs=[given] * n + [anywhere] * len(others),
        out_specs=[given] * n,
        out_shape=[shape(v.shape, v.dtype) for v in values],
        input_output_aliases={i: i for i in range(n)},
        name="after",
        compiler_params=pltpu.CompilerParams(vmem_limit_bytes=1 << 20),
    )(*values, *others)


def slots_of(ids):
    tokens = ids.shape[1]
    hit = jnp.where((ids[0:1] == 0) | (ids[1:2] == 0), 1.0, 0.0)
    hits = jnp.broadcast_to(hit, (SLOTS, tokens))
    before = jnp.where(iota((tokens, tokens), 0) < iota((tokens, tokens), 1), 1.0, 0.0)
    slot = mm(hits.astype(BF16), before.astype(BF16))
    place = jnp.where(slot > N_A - 0.5, slot + (PAD - N_A), slot)
    return jnp.where((hits > 0.5) & (place == iota((SLOTS, tokens), 0).astype(F32)), 1.0, 0.0)


def weights_of(ids, gates, chosen):
    gate = jnp.sum(jnp.where(ids == 0, gates, 0.0), axis=0, keepdims=True)
    return jnp.sum(chosen * gate, axis=1, keepdims=True)


def pack_kernel(
    xf, idf, gf, xb, idb, gb, grad, gain, send_a, send_b, keep_f, keep_x, keep_g, keep_w, place_f, place_b, ship_f, ship_b,
    own_a, own_b
):
    chosen_f = slots_of(idf[...])
    chosen_b = slots_of(idb[...])
    one_f = chosen_f.astype(BF16)
    one_b = chosen_b.astype(BF16)
    weight_f = weights_of(idf[...], gf[...], chosen_f)
    weight_b = weights_of(idb[...], gb[...], chosen_b)
    rows_f = mm(one_f, xf[...])
    rows_x = mm(one_b, xb[...])
    rows_g = mm(one_b, grad[...])

    def normal(rows):
        scale = lax.rsqrt(jnp.mean(rows * rows, axis=-1, keepdims=True) + EPS)
        return (rows * scale * gain[...]).astype(BF16)

    scaled = (rows_g * weight_b).astype(BF16)
    stacked = jnp.concatenate([normal(rows_f), normal(rows_x), scaled], axis=0)
    row, col = iota((2 * GATH, 3 * SLOTS), 0), iota((2 * GATH, 3 * SLOTS), 1)
    pick = jnp.zeros((2 * GATH, 3 * SLOTS), F32)
    for k in range(3):
        slot = col - SLOTS * k
        in_a = (slot >= 0) & (slot < N_A) & (row == slot + N_A * k)
        in_b = (slot >= PAD) & (slot < PAD + N_B) & (row == slot - PAD + N_B * k + GATH)
        pick = jnp.where(in_a | in_b, 1.0, pick)
    packed = mm(pick.astype(BF16), stacked)
    send_a[...] = packed[:GATH].astype(BF16)
    send_b[...] = packed[GATH:].astype(BF16)
    own_a[...] = packed[:GATH].astype(BF16)
    own_b[...] = packed[GATH:].astype(BF16)
    keep_f[...] = rows_f.astype(BF16)
    keep_x[...] = rows_x.astype(BF16)
    keep_g[...] = rows_g.astype(BF16)
    keep_w[...] = jnp.broadcast_to(weight_f, keep_w.shape)
    pad = jnp.zeros((SLOTS, 128 - xf.shape[0]), BF16)
    place_f[...] = jnp.concatenate([one_f, pad], axis=1)
    place_b[...] = jnp.concatenate([one_b, pad], axis=1)
    ship_f[...] = xf[...]
    ship_b[...] = grad[...]


def merge_rows(blocks, used, total):
    d = blocks[0].shape[1]
    stacked = jnp.concatenate([b[...] for b in blocks], axis=0)
    shape = (3 * total, 4 * GATH)
    row, col = iota(shape, 0), iota(shape, 1)
    pick = jnp.zeros(shape, F32)
    for k in range(3):
        for j in range(4):
            local = row - total * k - used * j
            good = (local >= 0) & (local < used) & (col == local + GATH * j + used * k)
            pick = jnp.where(good, 1.0, pick)
    moved = mm(pick.astype(BF16), stacked).astype(BF16)
    return [moved[total * k : total * (k + 1)] for k in range(3)], d


def merge_kernel(a0, a1, a2, a3, b0, b1, b2, b3, big_a, big_b):
    parts, d = merge_rows((a0, a1, a2, a3), N_A, ROWS_A)
    for k in range(3):
        big_a[:, k * d : (k + 1) * d] = parts[k]
    parts, d = merge_rows((b0, b1, b2, b3), N_B, ROWS_B)
    for k in range(3):
        big_b[:, k * d : (k + 1) * d] = parts[k]


def flip_kernel(up_own, up_other, down_own, down_other, after_merge, up, dn):
    half = up_own.shape[1]
    up[:half] = up_own[...].T
    up[half:] = up_other[...].T
    dn[:half] = down_own[...]
    dn[half:] = down_other[...]


def down_kernel(counts, hid, pg, dn, up, *refs):
    blocks = refs[len(refs) - len(counts) :]
    hidden, grad = hid[...], pg[...]
    tile = 768
    for t in range(0, dn.shape[1], tile):
        columns = slice(t, t + tile)
        first = mm(hidden, dn[:, columns])
        second = mm(grad, up[:, columns])
        start = 0
        for block in blocks:
            rows = block.shape[0] // 2
            block[:rows, columns] = first[start : start + rows].astype(BF16)
            block[rows:, columns] = second[start : start + rows].astype(BF16)
            start += rows


def down(hidden, pgrad, dn, up, counts, *others):
    d = dn.shape[1]
    kernel = functools.partial(down_kernel, counts)
    shapes = [out((2 * n, d)) for n in counts]
    return call(kernel, shapes, "down", after=(4 + len(others), len(others)))(
        hidden, pgrad, dn, up, *others
    )


def sum_rows(blocks, used, total):
    acc = blocks[0][...].astype(F32)
    for b in blocks[1:]:
        acc = acc + b[...].astype(F32)
    shape = (4 * SLOTS, 2 * total)
    row, col = iota(shape, 0), iota(shape, 1)
    pick = jnp.zeros(shape, F32)
    for j in range(4):
        for k in range(2):
            slot = row - SLOTS * j - PAD * k
            good = (slot >= 0) & (slot < used) & (col == slot + used * j + total * k)
            pick = jnp.where(good, 1.0, pick)
    moved = mm(pick.astype(BF16), acc.astype(BF16)).astype(BF16)
    return [moved[SLOTS * j : SLOTS * (j + 1)] for j in range(4)]


def sum_kernel(a0, a1, a2, a3, b0, b1, b2, b3, mine_up, mine_down, their_up, their_down, *outs):
    parts = sum_rows((a0, a1, a2, a3), N_A, ROWS_A) + sum_rows((b0, b1, b2, b3), N_B, ROWS_B)
    for ref, part in zip(outs, parts):
        ref[...] = part


def rows_kernel(
    a0, a1, a2, a3, b0, b1, b2, b3, keep_f, keep_x, keep_g, keep_w, place_f, place_b, gain, y_rows, dx_rows
):
    d = keep_f.shape[1]

    def total(refs):
        acc = refs[0][...].astype(F32)
        for r in refs[1:]:
            acc = acc + r[...].astype(F32)
        return acc.astype(BF16).astype(F32)

    part_a, part_b = total((a0, a1, a2, a3)), total((b0, b1, b2, b3))
    expert = jnp.concatenate([part_a[:PAD], part_b[:PAD]], axis=0)
    du = jnp.concatenate([part_a[PAD:], part_b[PAD:]], axis=0)
    y = keep_f[...].astype(F32) + keep_w[:, 0:1] * expert
    y_rows[:, :d] = y.astype(BF16)
    y_rows[:, d:] = place_f[...]
    x = keep_x[...].astype(F32)
    scale = lax.rsqrt(jnp.mean(x * x, axis=-1, keepdims=True) + EPS)
    h = du * gain[...]
    inner = jnp.mean(h * x, axis=-1, keepdims=True)
    dx = scale * h - x * (scale * scale * scale * inner)
    dx_rows[:, :d] = (keep_g[...].astype(F32) + dx).astype(BF16)
    dx_rows[:, d:] = place_b[...]


def place_kernel(base_f, y_rows, base_b, dx_rows, after_up, after_down, y_out, dx_out):
    tokens, d = base_f.shape
    ones = jnp.ones((SLOTS, 128), BF16)
    for base, rows, result in ((base_f, y_rows, y_out), (base_b, dx_rows, dx_out)):
        chosen = rows[:, d:]
        hit = mm(chosen, ones, ((0,), (0,)))[:tokens, 0:1]
        placed = mm(chosen, rows[:, :d], ((0,), (0,)))[:tokens]
        result[...] = jnp.where(hit > 0.5, placed, base[...].astype(F32)).astype(BF16)


def both(own_a, a, a_axis, own_b, b, b_axis, sign, wait=None):
    a1, a3 = shift(a[0], a_axis, sign), shift(a[2], a_axis, -sign)
    b1, b3 = shift(b[0], b_axis, sign), shift(b[2], b_axis, -sign)
    a2, b2 = a[1], b[1]
    if wait == "both":
        a2, b2 = after((a2, b2), (a1, b1))
    elif wait == "b":
        [b2] = after((b2,), (b1,), hbm=False)
    a2, b2 = shift(a2, a_axis, 2), shift(b2, b_axis, 2)
    return [own_a, a1, a2, a3], [own_b, b1, b2, b3]


def ring_gather(own, axis, first):
    ahead = shift(own, axis, 1)
    behind = shift(own, axis, -1)
    return [own, ahead, behind], [shift(ahead[:first], axis, 1), shift(behind[first:], axis, -1)]


def work(blocks, up, dn):
    rows = jnp.concatenate(blocks, axis=0)
    d = up.shape[1]
    rows_a, rows_b, grid_b = rows[:, :d], rows[:, d : 2 * d], rows[:, 2 * d :]
    pre_a = mm(rows_a, up, ((1,), (1,)))
    hidden_a = (pre_a * jax.nn.sigmoid(pre_a)).astype(BF16)
    pre_b = mm(rows_b, up, ((1,), (1,)))
    sigma = jax.nn.sigmoid(pre_b)
    hidden_b = (pre_b * sigma).astype(BF16)
    hidden_grad = mm(grid_b, dn, ((1,), (1,)))
    pgrad = (hidden_grad * sigma * (1.0 + pre_b * (1.0 - sigma))).astype(BF16)
    return hidden_a, (rows_b, grid_b, hidden_b, pgrad)


def on_device(
    fwd_in, fwd_ids, fwd_gate, bwd_in, bwd_ids, bwd_gate, bwd_grad, norm_gain, w_up, w_down
):
    tokens, d = fwd_in.shape[1:]
    send_a, send_b, keep_f, keep_x, keep_g, keep_w, place_f, place_b, base_f, base_b, own_a, own_b = call(
        pack_kernel,
        [pltpu.HBM((GATH, d), BF16)] * 2 + [out((SLOTS, d))] * 3 + [out((SLOTS, 128), F32)] + [out((SLOTS, 128))] * 2
        + [pltpu.HBM((tokens, d), BF16)] * 2 + [out((GATH, d))] * 2,
        "pack",
        62,
    )(
        fwd_in[0],
        fwd_ids[0].T,
        fwd_gate[0].T,
        bwd_in[0],
        bwd_ids[0].T,
        bwd_gate[0].T,
        bwd_grad[0],
        norm_gain,
    )
    up_own, down_own = w_up[0], w_down[0]
    half = up_own.shape[1]
    up_other, down_other = shift(up_own, "core", 1), shift(down_own, "core", 1)
    send_a, send_b = after((send_a, send_b), (up_other, down_other))
    a_blocks, b_blocks = both(own_a, [send_a] * 3, "x", own_b, [send_b] * 3, "y", 1, "both")
    big_a, big_b = call(merge_kernel, [out((ROWS_A, 3 * d)), out((ROWS_B, 3 * d))], "merge")(
        *a_blocks, *b_blocks
    )
    [base_f] = after((base_f,), (big_a,))
    base_f = shift(base_f, "pipe", 1)
    [base_b] = after((base_b,), (base_f,))
    base_b = shift(base_b, "pipe", -1)
    up, dn = call(flip_kernel, [out((2 * half, d))] * 2, "flip", after=(5, 1))(
        up_own, up_other, down_own, down_other, big_a
    )

    near_a, far_a = ring_gather(big_a, "y", 32)
    near_b, far_b = ring_gather(big_b, "x", 24)
    up, dn = after((up, dn), (far_b[0],), hbm=False)
    hidden_near, saved_near = work(near_a + near_b, up, dn)
    near = down(hidden_near, saved_near[3], dn, up, [ROWS_A] * 3 + [ROWS_B] * 3, base_f, base_b)
    hidden_far, saved_far = work(far_a + far_b, up, dn)
    far = down(hidden_far, saved_far[3], dn, up, [ROWS_A, ROWS_B])

    a_sums, b_sums = both(
        near[0], (near[1], far[0], near[2]), "y", near[3], (near[4], far[1], near[5]), "x", -1, "b"
    )
    saved_far = (*saved_far[:2], *after(saved_far[2:], (b_sums[1], b_sums[3], far[0])))
    over_rows = ((0,), (0,))

    def down_grad(saved, columns):
        return mm(saved[2][:, columns], saved[1], over_rows)

    def up_grad(saved, columns):
        return mm(saved[0], saved[3][:, columns], over_rows)

    theirs, mine = slice(half, None), slice(0, half)
    down_theirs = (down_grad(saved_near, theirs) + down_grad(saved_far, theirs)).astype(BF16)
    up_theirs = (up_grad(saved_near, theirs) + up_grad(saved_far, theirs)).astype(BF16)
    up_mine, down_mine = up_grad(saved_far, mine), down_grad(saved_far, mine)
    q = call(sum_kernel, [out((SLOTS, d))] * 8, "sums", after=(12, 4))(
        *a_sums, *b_sums, up_mine, down_mine, up_theirs, down_theirs
    )
    a_last, b_last = both(q[0], q[1:4], "x", q[4], q[5:8], "y", -1)
    y_rows, dx_rows = call(rows_kernel, [out((SLOTS, d + 128))] * 2, "rows")(
        *a_last, *b_last, keep_f, keep_x, keep_g, keep_w, place_f, place_b, norm_gain
    )
    up_theirs, down_theirs = after((up_theirs, down_theirs), (y_rows,))
    up_theirs, down_theirs = shift(up_theirs, "core", 1), shift(down_theirs, "core", 1)
    grad_down = (down_grad(saved_near, mine) + down_mine + down_theirs.astype(F32)).astype(BF16)
    grad_up = (up_grad(saved_near, mine) + up_mine + up_theirs.astype(F32)).astype(BF16)
    y_arrived = shift(y_rows, "pipe", 1)
    dx_arrived = shift(dx_rows, "pipe", -1)
    fwd_out, bwd_out = call(place_kernel, [out((tokens, d)), out((tokens, d))], "place", after=(6, 2))(
        base_f, y_arrived, base_b, dx_arrived, grad_up, grad_down
    )
    return (fwd_out[None], bwd_out[None], grad_up[None], grad_down[None])


def solution(mesh):
    chips = Mesh(mesh.devices.reshape(8, 4, 4, 2), ("pipe", "x", "y", "core"))
    expert = ("x", "y", "core")
    tokens = P("pipe", expert, None)
    return jax.shard_map(
        on_device,
        mesh=chips,
        in_specs=(tokens,) * 7 + (P("pipe", None), P("pipe", None, expert), P("pipe", expert, None)),
        out_specs=(tokens, tokens, P("pipe", None, expert), P("pipe", expert, None)),
        check_vma=False,
    )
```

```python
import functools

import jax
import jax.numpy as jnp
from jax import lax
from jax.experimental import pallas as pl
from jax.experimental.pallas import tpu as pltpu
from jax.sharding import Mesh, PartitionSpec as P

BF16 = jnp.bfloat16
F32 = jnp.float32
EPS = 1e-05
N_A = 13
N_B = 12
PAD = 16
SLOTS = 2 * PAD
GATH = 40
ROWS_A = 56
ROWS_B = 48


def shift(value, axis, by):
    count = lax.axis_size(axis)
    return lax.ppermute(value, axis, [(i, (i + by) % count) for i in range(count)])


def call(kernel, outs, name, vmem=20, after=None):
    count, unused = after or (0, 0)
    specs = {}
    if count:
        whole, later = pl.BlockSpec(memory_space=pltpu.VMEM), pl.BlockSpec(memory_space=pl.ANY)
        specs = {"in_specs": [whole] * (count - unused) + [later] * unused}
    return pl.pallas_call(
        kernel,
        **specs,
        out_shape=outs,
        name=name,
        compiler_params=pltpu.CompilerParams(vmem_limit_bytes=vmem * 1000 * 1024),
    )


def out(shape, dtype=BF16):
    return jax.ShapeDtypeStruct(shape, dtype)


def iota(shape, dim):
    return lax.broadcasted_iota(jnp.int32, shape, dim)


def mm(a, b, dims=((1,), (0,)), precision=None):
    return lax.dot_general(a, b, (dims, ((), ())), preferred_element_type=F32, precision=precision)


def after(values, others, hbm=True, left=()):
    n = len(values)
    place = pltpu.HBM if hbm else pl.ANY
    shape = pltpu.HBM if hbm else jax.ShapeDtypeStruct

    def nothing(*refs):
        pass

    given, anywhere = pl.BlockSpec(memory_space=place), pl.BlockSpec(memory_space=pl.ANY)
    slow = pl.BlockSpec(memory_space=pltpu.HBM)
    return pl.pallas_call(
        nothing,
        in_specs=[given] * n + [anywhere] * len(others) + [slow] * len(left),
        out_specs=[given] * n,
        out_shape=[shape(v.shape, v.dtype) for v in values],
        input_output_aliases={i: i for i in range(n)},
        name="after",
        compiler_params=pltpu.CompilerParams(vmem_limit_bytes=1 << 20),
    )(*values, *others, *left)


def slots_of(ids):
    tokens = ids.shape[1]
    hit = jnp.where((ids[0:1] == 0) | (ids[1:2] == 0), 1.0, 0.0)
    hits = jnp.broadcast_to(hit, (SLOTS, tokens))
    before = jnp.where(iota((tokens, tokens), 0) < iota((tokens, tokens), 1), 1.0, 0.0)
    slot = mm(hits.astype(BF16), before.astype(BF16))
    place = jnp.where(slot > N_A - 0.5, slot + (PAD - N_A), slot)
    return jnp.where((hits > 0.5) & (place == iota((SLOTS, tokens), 0).astype(F32)), 1.0, 0.0)


def weights_of(ids, gates, chosen):
    gate = jnp.sum(jnp.where(ids == 0, gates, 0.0), axis=0, keepdims=True)
    return jnp.sum(chosen * gate, axis=1, keepdims=True)


def pack_kernel(
    xf, idf, gf, xb, idb, gb, grad, gain, send_a, send_b, keep_f, keep_x, keep_g, keep_w, place_f, place_b, ship_f, ship_b,
    own_a, own_b
):
    chosen_f = slots_of(idf[...])
    chosen_b = slots_of(idb[...])
    one_f = chosen_f.astype(BF16)
    one_b = chosen_b.astype(BF16)
    weight_f = weights_of(idf[...], gf[...], chosen_f)
    weight_b = weights_of(idb[...], gb[...], chosen_b)
    rows_f = mm(one_f, xf[...])
    rows_x = mm(one_b, xb[...])
    rows_g = mm(one_b, grad[...])

    def normal(rows):
        scale = lax.rsqrt(jnp.mean(rows * rows, axis=-1, keepdims=True) + EPS)
        return (rows * scale * gain[...]).astype(BF16)

    scaled = (rows_g * weight_b).astype(BF16)
    stacked = jnp.concatenate([normal(rows_f), normal(rows_x), scaled], axis=0)
    row, col = iota((2 * GATH, 3 * SLOTS), 0), iota((2 * GATH, 3 * SLOTS), 1)
    pick = jnp.zeros((2 * GATH, 3 * SLOTS), F32)
    for k in range(3):
        slot = col - SLOTS * k
        in_a = (slot >= 0) & (slot < N_A) & (row == slot + N_A * k)
        in_b = (slot >= PAD) & (slot < PAD + N_B) & (row == slot - PAD + N_B * k + GATH)
        pick = jnp.where(in_a | in_b, 1.0, pick)
    packed = mm(pick.astype(BF16), stacked)
    send_a[...] = packed[:GATH].astype(BF16)
    send_b[...] = packed[GATH:].astype(BF16)
    own_a[...] = packed[:GATH].astype(BF16)
    own_b[...] = packed[GATH:].astype(BF16)
    keep_f[...] = rows_f.astype(BF16)
    keep_x[...] = rows_x.astype(BF16)
    keep_g[...] = rows_g.astype(BF16)
    keep_w[...] = jnp.broadcast_to(weight_f, keep_w.shape)
    pad = jnp.zeros((SLOTS, 128 - xf.shape[0]), BF16)
    place_f[...] = jnp.concatenate([one_f, pad], axis=1)
    place_b[...] = jnp.concatenate([one_b, pad], axis=1)
    ship_f[...] = xf[...]
    ship_b[...] = grad[...]


def merge_rows(blocks, used, total):
    d = blocks[0].shape[1]
    stacked = jnp.concatenate([b[...] for b in blocks], axis=0)
    shape = (3 * total, 4 * GATH)
    row, col = iota(shape, 0), iota(shape, 1)
    pick = jnp.zeros(shape, F32)
    for k in range(3):
        for j in range(4):
            local = row - total * k - used * j
            good = (local >= 0) & (local < used) & (col == local + GATH * j + used * k)
            pick = jnp.where(good, 1.0, pick)
    moved = mm(pick.astype(BF16), stacked).astype(BF16)
    return [moved[total * k : total * (k + 1)] for k in range(3)], d


def merge_kernel(a0, a1, a2, a3, b0, b1, b2, b3, big_a, big_b):
    parts, d = merge_rows((a0, a1, a2, a3), N_A, ROWS_A)
    for k in range(3):
        big_a[:, k * d : (k + 1) * d] = parts[k]
    parts, d = merge_rows((b0, b1, b2, b3), N_B, ROWS_B)
    for k in range(3):
        big_b[:, k * d : (k + 1) * d] = parts[k]


def flip_kernel(up_own, up_other, down_own, down_other, after_merge, up, dn):
    half = up_own.shape[1]
    up[:half] = up_own[...].T
    up[half:] = up_other[...].T
    dn[:half] = down_own[...]
    dn[half:] = down_other[...]


def down_kernel(counts, hid, pg, dn, up, *refs):
    blocks = refs[len(refs) - len(counts) :]
    hidden, grad = hid[...], pg[...]
    tile = 768
    for t in range(0, dn.shape[1], tile):
        columns = slice(t, t + tile)
        first = mm(hidden, dn[:, columns])
        second = mm(grad, up[:, columns])
        start = 0
        for block in blocks:
            rows = block.shape[0] // 2
            block[:rows, columns] = first[start : start + rows].astype(BF16)
            block[rows:, columns] = second[start : start + rows].astype(BF16)
            start += rows


def down(hidden, pgrad, dn, up, counts, *others, shape=out):
    d = dn.shape[1]
    kernel = functools.partial(down_kernel, counts)
    shapes = [shape((2 * n, d), BF16) for n in counts]
    return call(kernel, shapes, "down", after=(4 + len(others), len(others)))(
        hidden, pgrad, dn, up, *others
    )


def sum_rows(blocks, used, total):
    acc = blocks[0][...].astype(F32)
    for b in blocks[1:]:
        acc = acc + b[...].astype(F32)
    shape = (4 * SLOTS, 2 * total)
    row, col = iota(shape, 0), iota(shape, 1)
    pick = jnp.zeros(shape, F32)
    for j in range(4):
        for k in range(2):
            slot = row - SLOTS * j - PAD * k
            good = (slot >= 0) & (slot < used) & (col == slot + used * j + total * k)
            pick = jnp.where(good, 1.0, pick)
    moved = mm(pick.astype(BF16), acc.astype(BF16)).astype(BF16)
    return [moved[SLOTS * j : SLOTS * (j + 1)] for j in range(4)]


def sum_kernel(a0, a1, a2, a3, b0, b1, b2, b3, mine_up, mine_down, their_up, their_down, *outs):
    parts = sum_rows((a0, a1, a2, a3), N_A, ROWS_A) + sum_rows((b0, b1, b2, b3), N_B, ROWS_B)
    for ref, part in zip(outs, parts):
        ref[...] = part


def rows_kernel(
    a0, a1, a2, a3, b0, b1, b2, b3, keep_f, keep_x, keep_g, keep_w, place_f, place_b, gain, y_rows, dx_rows
):
    d = keep_f.shape[1]

    def total(refs):
        acc = refs[0][...].astype(F32)
        for r in refs[1:]:
            acc = acc + r[...].astype(F32)
        return acc.astype(BF16).astype(F32)

    part_a, part_b = total((a0, a1, a2, a3)), total((b0, b1, b2, b3))
    expert = jnp.concatenate([part_a[:PAD], part_b[:PAD]], axis=0)
    du = jnp.concatenate([part_a[PAD:], part_b[PAD:]], axis=0)
    y = keep_f[...].astype(F32) + keep_w[:, 0:1] * expert
    y_rows[:, :d] = y.astype(BF16)
    y_rows[:, d:] = place_f[...]
    x = keep_x[...].astype(F32)
    scale = lax.rsqrt(jnp.mean(x * x, axis=-1, keepdims=True) + EPS)
    h = du * gain[...]
    inner = jnp.mean(h * x, axis=-1, keepdims=True)
    dx = scale * h - x * (scale * scale * scale * inner)
    dx_rows[:, :d] = (keep_g[...].astype(F32) + dx).astype(BF16)
    dx_rows[:, d:] = place_b[...]


def place_kernel(base_f, y_rows, base_b, dx_rows, after_up, after_down, y_out, dx_out):
    tokens, d = base_f.shape
    ones = jnp.ones((SLOTS, 128), BF16)
    for base, rows, result in ((base_f, y_rows, y_out), (base_b, dx_rows, dx_out)):
        chosen = rows[:, d:]
        hit = mm(chosen, ones, ((0,), (0,)))[:tokens, 0:1]
        placed = mm(chosen, rows[:, :d], ((0,), (0,)))[:tokens]
        result[...] = jnp.where(hit > 0.5, placed, base[...].astype(F32)).astype(BF16)


def both(own_a, a, a_axis, own_b, b, b_axis, sign, wait=None):
    a1, a3 = shift(a[0], a_axis, sign), shift(a[2], a_axis, -sign)
    b1, b3 = shift(b[0], b_axis, sign), shift(b[2], b_axis, -sign)
    a2, b2 = a[1], b[1]
    if wait == "both":
        a2, b2 = after((a2, b2), (a1, b1))
    elif wait == "a":
        [a2] = after((a2,), (a1,))
    a2, b2 = shift(a2, a_axis, 2), shift(b2, b_axis, 2)
    return [own_a, a1, a2, a3], [own_b, b1, b2, b3]


def ring_gather(own, axis, first):
    ahead = shift(own, axis, 1)
    behind = shift(own, axis, -1)
    return [own, ahead, behind], [shift(ahead[:first], axis, 1), shift(behind[first:], axis, -1)]


def work(blocks, up, dn):
    rows = jnp.concatenate(blocks, axis=0)
    d = up.shape[1]
    rows_a, rows_b, grid_b = rows[:, :d], rows[:, d : 2 * d], rows[:, 2 * d :]
    pre_a = mm(rows_a, up, ((1,), (1,)))
    hidden_a = (pre_a * jax.nn.sigmoid(pre_a)).astype(BF16)
    pre_b = mm(rows_b, up, ((1,), (1,)))
    sigma = jax.nn.sigmoid(pre_b)
    hidden_b = (pre_b * sigma).astype(BF16)
    hidden_grad = mm(grid_b, dn, ((1,), (1,)))
    pgrad = (hidden_grad * sigma * (1.0 + pre_b * (1.0 - sigma))).astype(BF16)
    return hidden_a, (rows_b, grid_b, hidden_b, pgrad)


def on_device(
    fwd_in, fwd_ids, fwd_gate, bwd_in, bwd_ids, bwd_gate, bwd_grad, norm_gain, w_up, w_down
):
    tokens, d = fwd_in.shape[1:]
    send_a, send_b, keep_f, keep_x, keep_g, keep_w, place_f, place_b, base_f, base_b, own_a, own_b = call(
        pack_kernel,
        [pltpu.HBM((GATH, d), BF16)] * 2 + [out((SLOTS, d))] * 3 + [out((SLOTS, 128), F32)] + [out((SLOTS, 128))] * 2
        + [pltpu.HBM((tokens, d), BF16)] * 2 + [out((GATH, d))] * 2,
        "pack",
        62,
    )(
        fwd_in[0],
        fwd_ids[0].T,
        fwd_gate[0].T,
        bwd_in[0],
        bwd_ids[0].T,
        bwd_gate[0].T,
        bwd_grad[0],
        norm_gain,
    )
    up_own, down_own = w_up[0], w_down[0]
    half = up_own.shape[1]
    up_other, down_other = shift(up_own, "core", 1), shift(down_own, "core", 1)
    send_a, send_b = after((send_a, send_b), (up_other, down_other))
    a_blocks, b_blocks = both(own_a, [send_a] * 3, "x", own_b, [send_b] * 3, "y", 1, "both")
    big_a, big_b = call(merge_kernel, [out((ROWS_A, 3 * d)), out((ROWS_B, 3 * d))], "merge")(
        *a_blocks, *b_blocks
    )
    [base_f] = after((base_f,), (big_a,))
    base_f = shift(base_f, "pipe", 1)
    [base_b] = after((base_b,), (base_f,))
    base_b = shift(base_b, "pipe", -1)
    up, dn = call(flip_kernel, [out((2 * half, d))] * 2, "flip", after=(5, 1))(
        up_own, up_other, down_own, down_other, big_a
    )

    near_a, far_a = ring_gather(big_a, "y", 32)
    near_b, far_b = ring_gather(big_b, "x", 24)
    up, dn = after((up, dn), (far_b[0],), hbm=False)
    hidden_near, saved_near = work(near_a + near_b, up, dn)
    near = down(hidden_near, saved_near[3], dn, up, [ROWS_A] * 3 + [ROWS_B] * 3, base_f, base_b)
    hidden_far, saved_far = work(far_a + far_b, up, dn)
    far = down(hidden_far, saved_far[3], dn, up, [ROWS_A, ROWS_B], shape=pltpu.HBM)

    a_sums, b_sums = both(
        near[0], (near[1], far[0], near[2]), "y", near[3], (near[4], far[1], near[5]), "x", -1, "a"
    )
    saved_far = (*saved_far[:2], *after(saved_far[2:], (a_sums[1],), left=(far[0],)))
    over_rows = ((0,), (0,))

    def down_grad(saved, columns):
        return mm(saved[2][:, columns], saved[1], over_rows)

    def up_grad(saved, columns):
        return mm(saved[0], saved[3][:, columns], over_rows)

    theirs, mine = slice(half, None), slice(0, half)
    down_theirs = (down_grad(saved_near, theirs) + down_grad(saved_far, theirs)).astype(BF16)
    up_theirs = (up_grad(saved_near, theirs) + up_grad(saved_far, theirs)).astype(BF16)
    up_mine, down_mine = up_grad(saved_far, mine), down_grad(saved_far, mine)
    q = call(sum_kernel, [out((SLOTS, d))] * 8, "sums", after=(12, 4))(
        *a_sums, *b_sums, up_mine, down_mine, up_theirs, down_theirs
    )
    a_last, b_last = both(q[0], q[1:4], "x", q[4], q[5:8], "y", -1)
    y_rows, dx_rows = call(rows_kernel, [out((SLOTS, d + 128))] * 2, "rows")(
        *a_last, *b_last, keep_f, keep_x, keep_g, keep_w, place_f, place_b, norm_gain
    )
    up_theirs, down_theirs = after((up_theirs, down_theirs), (y_rows,))
    up_theirs, down_theirs = shift(up_theirs, "core", 1), shift(down_theirs, "core", 1)
    grad_down = (down_grad(saved_near, mine) + down_mine + down_theirs.astype(F32)).astype(BF16)
    grad_up = (up_grad(saved_near, mine) + up_mine + up_theirs.astype(F32)).astype(BF16)
    y_arrived = shift(y_rows, "pipe", 1)
    dx_arrived = shift(dx_rows, "pipe", -1)
    fwd_out, bwd_out = call(place_kernel, [out((tokens, d)), out((tokens, d))], "place", after=(6, 2))(
        base_f, y_arrived, base_b, dx_arrived, grad_up, grad_down
    )
    return (fwd_out[None], bwd_out[None], grad_up[None], grad_down[None])


def solution(mesh):
    chips = Mesh(mesh.devices.reshape(8, 4, 4, 2), ("pipe", "x", "y", "core"))
    expert = ("x", "y", "core")
    tokens = P("pipe", expert, None)
    return jax.shard_map(
        on_device,
        mesh=chips,
        in_specs=(tokens,) * 7 + (P("pipe", None), P("pipe", None, expert), P("pipe", expert, None)),
        out_specs=(tokens, tokens, P("pipe", None, expert), P("pipe", expert, None)),
        check_vma=False,
    )
```

```python
import functools

import jax
import jax.numpy as jnp
from jax import lax
from jax.experimental import pallas as pl
from jax.experimental.pallas import tpu as pltpu
from jax.sharding import Mesh, PartitionSpec as P

BF16 = jnp.bfloat16
F32 = jnp.float32
EPS = 1e-05
N_A = 13
N_B = 12
PAD = 16
SLOTS = 2 * PAD
GATH = 40
ROWS_A = 56
ROWS_B = 48


def shift(value, axis, by):
    count = lax.axis_size(axis)
    return lax.ppermute(value, axis, [(i, (i + by) % count) for i in range(count)])


def call(kernel, outs, name, vmem=20, after=None):
    count, unused = after or (0, 0)
    specs = {}
    if count:
        whole, later = pl.BlockSpec(memory_space=pltpu.VMEM), pl.BlockSpec(memory_space=pl.ANY)
        specs = {"in_specs": [whole] * (count - unused) + [later] * unused}
    return pl.pallas_call(
        kernel,
        **specs,
        out_shape=outs,
        name=name,
        compiler_params=pltpu.CompilerParams(vmem_limit_bytes=vmem * 1000 * 1024),
    )


def out(shape, dtype=BF16):
    return jax.ShapeDtypeStruct(shape, dtype)


def iota(shape, dim):
    return lax.broadcasted_iota(jnp.int32, shape, dim)


def mm(a, b, dims=((1,), (0,)), precision=None):
    return lax.dot_general(a, b, (dims, ((), ())), preferred_element_type=F32, precision=precision)


def after(values, others, hbm=True, left=()):
    n = len(values)
    place = pltpu.HBM if hbm else pl.ANY
    shape = pltpu.HBM if hbm else jax.ShapeDtypeStruct

    def nothing(*refs):
        pass

    given, anywhere = pl.BlockSpec(memory_space=place), pl.BlockSpec(memory_space=pl.ANY)
    slow = pl.BlockSpec(memory_space=pltpu.HBM)
    return pl.pallas_call(
        nothing,
        in_specs=[given] * n + [anywhere] * len(others) + [slow] * len(left),
        out_specs=[given] * n,
        out_shape=[shape(v.shape, v.dtype) for v in values],
        input_output_aliases={i: i for i in range(n)},
        name="after",
        compiler_params=pltpu.CompilerParams(vmem_limit_bytes=1 << 20),
    )(*values, *others, *left)


def slots_of(ids):
    tokens = ids.shape[1]
    hit = jnp.where((ids[0:1] == 0) | (ids[1:2] == 0), 1.0, 0.0)
    hits = jnp.broadcast_to(hit, (SLOTS, tokens))
    before = jnp.where(iota((tokens, tokens), 0) < iota((tokens, tokens), 1), 1.0, 0.0)
    slot = mm(hits.astype(BF16), before.astype(BF16))
    place = jnp.where(slot > N_A - 0.5, slot + (PAD - N_A), slot)
    return jnp.where((hits > 0.5) & (place == iota((SLOTS, tokens), 0).astype(F32)), 1.0, 0.0)


def weights_of(ids, gates, chosen):
    gate = jnp.sum(jnp.where(ids == 0, gates, 0.0), axis=0, keepdims=True)
    return jnp.sum(chosen * gate, axis=1, keepdims=True)


def pack_kernel(
    xf, idf, gf, xb, idb, gb, grad, gain, send_a, send_b, keep_f, keep_x, keep_g, keep_w, place_f, place_b, ship_f, ship_b,
    own_a, own_b
):
    chosen_f = slots_of(idf[...])
    chosen_b = slots_of(idb[...])
    one_f = chosen_f.astype(BF16)
    one_b = chosen_b.astype(BF16)
    weight_f = weights_of(idf[...], gf[...], chosen_f)
    weight_b = weights_of(idb[...], gb[...], chosen_b)
    rows_f = mm(one_f, xf[...])
    rows_x = mm(one_b, xb[...])
    rows_g = mm(one_b, grad[...])

    def normal(rows):
        scale = lax.rsqrt(jnp.mean(rows * rows, axis=-1, keepdims=True) + EPS)
        return (rows * scale * gain[...]).astype(BF16)

    scaled = (rows_g * weight_b).astype(BF16)
    stacked = jnp.concatenate([normal(rows_f), normal(rows_x), scaled], axis=0)
    row, col = iota((2 * GATH, 3 * SLOTS), 0), iota((2 * GATH, 3 * SLOTS), 1)
    pick = jnp.zeros((2 * GATH, 3 * SLOTS), F32)
    for k in range(3):
        slot = col - SLOTS * k
        in_a = (slot >= 0) & (slot < N_A) & (row == slot + N_A * k)
        in_b = (slot >= PAD) & (slot < PAD + N_B) & (row == slot - PAD + N_B * k + GATH)
        pick = jnp.where(in_a | in_b, 1.0, pick)
    packed = mm(pick.astype(BF16), stacked)
    send_a[...] = packed[:GATH].astype(BF16)
    send_b[...] = packed[GATH:].astype(BF16)
    own_a[...] = packed[:GATH].astype(BF16)
    own_b[...] = packed[GATH:].astype(BF16)
    keep_f[...] = rows_f.astype(BF16)
    keep_x[...] = rows_x.astype(BF16)
    keep_g[...] = rows_g.astype(BF16)
    keep_w[...] = jnp.broadcast_to(weight_f, keep_w.shape)
    pad = jnp.zeros((SLOTS, 128 - xf.shape[0]), BF16)
    place_f[...] = jnp.concatenate([one_f, pad], axis=1)
    place_b[...] = jnp.concatenate([one_b, pad], axis=1)
    ship_f[...] = xf[...]
    ship_b[...] = grad[...]


def merge_rows(blocks, used, total):
    d = blocks[0].shape[1]
    stacked = jnp.concatenate([b[...] for b in blocks], axis=0)
    shape = (3 * total, 4 * GATH)
    row, col = iota(shape, 0), iota(shape, 1)
    pick = jnp.zeros(shape, F32)
    for k in range(3):
        for j in range(4):
            local = row - total * k - used * j
            good = (local >= 0) & (local < used) & (col == local + GATH * j + used * k)
            pick = jnp.where(good, 1.0, pick)
    moved = mm(pick.astype(BF16), stacked).astype(BF16)
    return [moved[total * k : total * (k + 1)] for k in range(3)], d


def merge_kernel(a0, a1, a2, a3, b0, b1, b2, b3, big_a, big_b):
    parts, d = merge_rows((a0, a1, a2, a3), N_A, ROWS_A)
    for k in range(3):
        big_a[:, k * d : (k + 1) * d] = parts[k]
    parts, d = merge_rows((b0, b1, b2, b3), N_B, ROWS_B)
    for k in range(3):
        big_b[:, k * d : (k + 1) * d] = parts[k]


def flip_kernel(up_own, up_other, down_own, down_other, after_merge, up, dn):
    half = up_own.shape[1]
    up[:half] = up_own[...].T
    up[half:] = up_other[...].T
    dn[:half] = down_own[...]
    dn[half:] = down_other[...]


def down_kernel(counts, hid, pg, dn, up, *refs):
    blocks = refs[len(refs) - len(counts) :]
    hidden, grad = hid[...], pg[...]
    tile = 768
    for t in range(0, dn.shape[1], tile):
        columns = slice(t, t + tile)
        first = mm(hidden, dn[:, columns])
        second = mm(grad, up[:, columns])
        start = 0
        for block in blocks:
            rows = block.shape[0] // 2
            block[:rows, columns] = first[start : start + rows].astype(BF16)
            block[rows:, columns] = second[start : start + rows].astype(BF16)
            start += rows


def down(hidden, pgrad, dn, up, counts, *others, shape=out):
    d = dn.shape[1]
    kernel = functools.partial(down_kernel, counts)
    shapes = [shape((2 * n, d), BF16) for n in counts]
    return call(kernel, shapes, "down", after=(4 + len(others), len(others)))(
        hidden, pgrad, dn, up, *others
    )


def sum_rows(blocks, used, total):
    acc = blocks[0][...].astype(F32)
    for b in blocks[1:]:
        acc = acc + b[...].astype(F32)
    shape = (4 * SLOTS, 2 * total)
    row, col = iota(shape, 0), iota(shape, 1)
    pick = jnp.zeros(shape, F32)
    for j in range(4):
        for k in range(2):
            slot = row - SLOTS * j - PAD * k
            good = (slot >= 0) & (slot < used) & (col == slot + used * j + total * k)
            pick = jnp.where(good, 1.0, pick)
    moved = mm(pick.astype(BF16), acc.astype(BF16)).astype(BF16)
    return [moved[SLOTS * j : SLOTS * (j + 1)] for j in range(4)]


def sum_kernel(a0, a1, a2, a3, b0, b1, b2, b3, their_up, their_down, *outs):
    parts = sum_rows((a0, a1, a2, a3), N_A, ROWS_A) + sum_rows((b0, b1, b2, b3), N_B, ROWS_B)
    for ref, part in zip(outs, parts):
        ref[...] = part


def rows_kernel(
    a0, a1, a2, a3, b0, b1, b2, b3, keep_f, keep_x, keep_g, keep_w, place_f, place_b, gain, y_rows, dx_rows
):
    d = keep_f.shape[1]

    def total(refs):
        acc = refs[0][...].astype(F32)
        for r in refs[1:]:
            acc = acc + r[...].astype(F32)
        return acc.astype(BF16).astype(F32)

    part_a, part_b = total((a0, a1, a2, a3)), total((b0, b1, b2, b3))
    expert = jnp.concatenate([part_a[:PAD], part_b[:PAD]], axis=0)
    du = jnp.concatenate([part_a[PAD:], part_b[PAD:]], axis=0)
    y = keep_f[...].astype(F32) + keep_w[:, 0:1] * expert
    y_rows[:, :d] = y.astype(BF16)
    y_rows[:, d:] = place_f[...]
    x = keep_x[...].astype(F32)
    scale = lax.rsqrt(jnp.mean(x * x, axis=-1, keepdims=True) + EPS)
    h = du * gain[...]
    inner = jnp.mean(h * x, axis=-1, keepdims=True)
    dx = scale * h - x * (scale * scale * scale * inner)
    dx_rows[:, :d] = (keep_g[...].astype(F32) + dx).astype(BF16)
    dx_rows[:, d:] = place_b[...]


def place_kernel(base_f, y_rows, base_b, dx_rows, after_up, after_down, y_out, dx_out):
    tokens, d = base_f.shape
    ones = jnp.ones((SLOTS, 128), BF16)
    for base, rows, result in ((base_f, y_rows, y_out), (base_b, dx_rows, dx_out)):
        chosen = rows[:, d:]
        hit = mm(chosen, ones, ((0,), (0,)))[:tokens, 0:1]
        placed = mm(chosen, rows[:, :d], ((0,), (0,)))[:tokens]
        result[...] = jnp.where(hit > 0.5, placed, base[...].astype(F32)).astype(BF16)


def both(own_a, a, a_axis, own_b, b, b_axis, sign, wait=None):
    a1, a3 = shift(a[0], a_axis, sign), shift(a[2], a_axis, -sign)
    b1, b3 = shift(b[0], b_axis, sign), shift(b[2], b_axis, -sign)
    a2, b2 = a[1], b[1]
    if wait == "a":
        [a2] = after((a2,), (a1,))
    a2, b2 = shift(a2, a_axis, 2), shift(b2, b_axis, 2)
    return [own_a, a1, a2, a3], [own_b, b1, b2, b3]


def ring_gather(own, axis, first):
    ahead = shift(own, axis, 1)
    behind = shift(own, axis, -1)
    return [own, ahead, behind], [shift(ahead[:first], axis, 1), shift(behind[first:], axis, -1)]


def work(blocks, up, dn):
    rows = jnp.concatenate(blocks, axis=0)
    d = up.shape[1]
    rows_a, rows_b, grid_b = rows[:, :d], rows[:, d : 2 * d], rows[:, 2 * d :]
    pre_a = mm(rows_a, up, ((1,), (1,)))
    hidden_a = (pre_a * jax.nn.sigmoid(pre_a)).astype(BF16)
    pre_b = mm(rows_b, up, ((1,), (1,)))
    sigma = jax.nn.sigmoid(pre_b)
    hidden_b = (pre_b * sigma).astype(BF16)
    hidden_grad = mm(grid_b, dn, ((1,), (1,)))
    pgrad = (hidden_grad * sigma * (1.0 + pre_b * (1.0 - sigma))).astype(BF16)
    return hidden_a, (rows_b, grid_b, hidden_b, pgrad)


def on_device(
    fwd_in, fwd_ids, fwd_gate, bwd_in, bwd_ids, bwd_gate, bwd_grad, norm_gain, w_up, w_down
):
    tokens, d = fwd_in.shape[1:]
    send_a, send_b, keep_f, keep_x, keep_g, keep_w, place_f, place_b, base_f, base_b, own_a, own_b = call(
        pack_kernel,
        [pltpu.HBM((GATH, d), BF16)] * 2 + [out((SLOTS, d))] * 3 + [out((SLOTS, 128), F32)] + [out((SLOTS, 128))] * 2
        + [pltpu.HBM((tokens, d), BF16)] * 2 + [out((GATH, d))] * 2,
        "pack",
        62,
    )(
        fwd_in[0],
        fwd_ids[0].T,
        fwd_gate[0].T,
        bwd_in[0],
        bwd_ids[0].T,
        bwd_gate[0].T,
        bwd_grad[0],
        norm_gain,
    )
    up_own, down_own = w_up[0], w_down[0]
    half = up_own.shape[1]
    up_other, down_other = shift(up_own, "core", 1), shift(down_own, "core", 1)
    send_a, send_b = after((send_a, send_b), (up_other, down_other))
    a_blocks, b_blocks = both(own_a, [send_a] * 3, "x", own_b, [send_b] * 3, "y", 1)
    big_a, big_b = call(merge_kernel, [out((ROWS_A, 3 * d)), out((ROWS_B, 3 * d))], "merge")(
        *a_blocks, *b_blocks
    )
    [base_f] = after((base_f,), (big_a,))
    base_f = shift(base_f, "pipe", 1)
    [base_b] = after((base_b,), (base_f,))
    base_b = shift(base_b, "pipe", -1)
    up, dn = call(flip_kernel, [out((2 * half, d))] * 2, "flip", after=(5, 1))(
        up_own, up_other, down_own, down_other, big_a
    )

    near_a, far_a = ring_gather(big_a, "y", 32)
    near_b, far_b = ring_gather(big_b, "x", 24)
    up, dn = after((up, dn), (far_b[0],), hbm=False)
    hidden_near, saved_near = work(near_a + near_b, up, dn)
    near = down(hidden_near, saved_near[3], dn, up, [ROWS_A] * 3 + [ROWS_B] * 3, base_f, base_b)
    hidden_far, saved_far = work(far_a + far_b, up, dn)
    far = down(hidden_far, saved_far[3], dn, up, [ROWS_A, ROWS_B], shape=pltpu.HBM)

    a_sums, b_sums = both(
        near[0], (near[1], far[0], near[2]), "y", near[3], (near[4], far[1], near[5]), "x", -1, "a"
    )
    saved_far = (*saved_far[:2], *after(saved_far[2:], (a_sums[1],), left=(far[0],)))
    over_rows = ((0,), (0,))

    def down_grad(saved, columns):
        return mm(saved[2][:, columns], saved[1], over_rows)

    def up_grad(saved, columns):
        return mm(saved[0], saved[3][:, columns], over_rows)

    theirs, mine = slice(half, None), slice(0, half)
    down_theirs = (down_grad(saved_near, theirs) + down_grad(saved_far, theirs)).astype(BF16)
    up_theirs = (up_grad(saved_near, theirs) + up_grad(saved_far, theirs)).astype(BF16)
    q = call(sum_kernel, [out((SLOTS, d))] * 8, "sums", after=(10, 2))(
        *a_sums, *b_sums, up_theirs, down_theirs
    )
    a_last, b_last = both(q[0], q[1:4], "x", q[4], q[5:8], "y", -1)
    y_rows, dx_rows = call(rows_kernel, [out((SLOTS, d + 128))] * 2, "rows")(
        *a_last, *b_last, keep_f, keep_x, keep_g, keep_w, place_f, place_b, norm_gain
    )
    up_theirs, down_theirs = after((up_theirs, down_theirs), (y_rows,))
    up_theirs, down_theirs = shift(up_theirs, "core", 1), shift(down_theirs, "core", 1)
    saved_far = (*saved_far[:2], *after(saved_far[2:], (up_theirs,), hbm=False))
    down_mine, up_mine = down_grad(saved_far, mine), up_grad(saved_far, mine)
    grad_down = (down_grad(saved_near, mine) + down_mine + down_theirs.astype(F32)).astype(BF16)
    grad_up = (up_grad(saved_near, mine) + up_mine + up_theirs.astype(F32)).astype(BF16)
    y_arrived = shift(y_rows, "pipe", 1)
    dx_arrived = shift(dx_rows, "pipe", -1)
    fwd_out, bwd_out = call(place_kernel, [out((tokens, d)), out((tokens, d))], "place", after=(6, 2))(
        base_f, y_arrived, base_b, dx_arrived, grad_up, grad_down
    )
    return (fwd_out[None], bwd_out[None], grad_up[None], grad_down[None])


def solution(mesh):
    chips = Mesh(mesh.devices.reshape(8, 4, 4, 2), ("pipe", "x", "y", "core"))
    expert = ("x", "y", "core")
    tokens = P("pipe", expert, None)
    return jax.shard_map(
        on_device,
        mesh=chips,
        in_specs=(tokens,) * 7 + (P("pipe", None), P("pipe", None, expert), P("pipe", expert, None)),
        out_specs=(tokens, tokens, P("pipe", None, expert), P("pipe", expert, None)),
        check_vma=False,
    )
```

```python
import functools

import jax
import jax.numpy as jnp
from jax import lax
from jax.experimental import pallas as pl
from jax.experimental.pallas import tpu as pltpu
from jax.sharding import Mesh, PartitionSpec as P

BF16 = jnp.bfloat16
F32 = jnp.float32
EPS = 1e-05
N_A = 13
N_B = 12
PAD = 16
SLOTS = 2 * PAD
GATH = 40
ROWS_A = 56
ROWS_B = 48


def shift(value, axis, by):
    count = lax.axis_size(axis)
    return lax.ppermute(value, axis, [(i, (i + by) % count) for i in range(count)])


def call(kernel, outs, name, vmem=20, after=None):
    count, unused = after or (0, 0)
    specs = {}
    if count:
        whole, later = pl.BlockSpec(memory_space=pltpu.VMEM), pl.BlockSpec(memory_space=pl.ANY)
        specs = {"in_specs": [whole] * (count - unused) + [later] * unused}
    return pl.pallas_call(
        kernel,
        **specs,
        out_shape=outs,
        name=name,
        compiler_params=pltpu.CompilerParams(vmem_limit_bytes=vmem * 1000 * 1024),
    )


def out(shape, dtype=BF16):
    return jax.ShapeDtypeStruct(shape, dtype)


def iota(shape, dim):
    return lax.broadcasted_iota(jnp.int32, shape, dim)


def mm(a, b, dims=((1,), (0,)), precision=None):
    return lax.dot_general(a, b, (dims, ((), ())), preferred_element_type=F32, precision=precision)


def after(values, others, hbm=True, left=()):
    n = len(values)
    place = pltpu.HBM if hbm else pl.ANY
    shape = pltpu.HBM if hbm else jax.ShapeDtypeStruct

    def nothing(*refs):
        pass

    given, anywhere = pl.BlockSpec(memory_space=place), pl.BlockSpec(memory_space=pl.ANY)
    slow = pl.BlockSpec(memory_space=pltpu.HBM)
    return pl.pallas_call(
        nothing,
        in_specs=[given] * n + [anywhere] * len(others) + [slow] * len(left),
        out_specs=[given] * n,
        out_shape=[shape(v.shape, v.dtype) for v in values],
        input_output_aliases={i: i for i in range(n)},
        name="after",
        compiler_params=pltpu.CompilerParams(vmem_limit_bytes=1 << 20),
    )(*values, *others, *left)


def slots_of(ids):
    tokens = ids.shape[1]
    hit = jnp.where((ids[0:1] == 0) | (ids[1:2] == 0), 1.0, 0.0)
    hits = jnp.broadcast_to(hit, (SLOTS, tokens))
    before = jnp.where(iota((tokens, tokens), 0) < iota((tokens, tokens), 1), 1.0, 0.0)
    slot = mm(hits.astype(BF16), before.astype(BF16))
    place = jnp.where(slot > N_A - 0.5, slot + (PAD - N_A), slot)
    return jnp.where((hits > 0.5) & (place == iota((SLOTS, tokens), 0).astype(F32)), 1.0, 0.0)


def weights_of(ids, gates, chosen):
    gate = jnp.sum(jnp.where(ids == 0, gates, 0.0), axis=0, keepdims=True)
    return jnp.sum(chosen * gate, axis=1, keepdims=True)


def pack_kernel(
    xf, idf, gf, xb, idb, gb, grad, gain, send_a, send_b, keep_f, keep_x, keep_g, keep_w, place_f, place_b, ship_f, ship_b,
    own_a, own_b
):
    chosen_f = slots_of(idf[...])
    chosen_b = slots_of(idb[...])
    one_f = chosen_f.astype(BF16)
    one_b = chosen_b.astype(BF16)
    weight_f = weights_of(idf[...], gf[...], chosen_f)
    weight_b = weights_of(idb[...], gb[...], chosen_b)
    rows_f = mm(one_f, xf[...])
    rows_x = mm(one_b, xb[...])
    rows_g = mm(one_b, grad[...])

    def normal(rows):
        scale = lax.rsqrt(jnp.mean(rows * rows, axis=-1, keepdims=True) + EPS)
        return (rows * scale * gain[...]).astype(BF16)

    scaled = (rows_g * weight_b).astype(BF16)
    stacked = jnp.concatenate([normal(rows_f), normal(rows_x), scaled], axis=0)
    row, col = iota((2 * GATH, 3 * SLOTS), 0), iota((2 * GATH, 3 * SLOTS), 1)
    pick = jnp.zeros((2 * GATH, 3 * SLOTS), F32)
    for k in range(3):
        slot = col - SLOTS * k
        in_a = (slot >= 0) & (slot < N_A) & (row == slot + N_A * k)
        in_b = (slot >= PAD) & (slot < PAD + N_B) & (row == slot - PAD + N_B * k + GATH)
        pick = jnp.where(in_a | in_b, 1.0, pick)
    packed = mm(pick.astype(BF16), stacked)
    send_a[...] = packed[:GATH].astype(BF16)
    send_b[...] = packed[GATH:].astype(BF16)
    own_a[...] = packed[:GATH].astype(BF16)
    own_b[...] = packed[GATH:].astype(BF16)
    keep_f[...] = rows_f.astype(BF16)
    keep_x[...] = rows_x.astype(BF16)
    keep_g[...] = rows_g.astype(BF16)
    keep_w[...] = jnp.broadcast_to(weight_f, keep_w.shape)
    pad = jnp.zeros((SLOTS, 128 - xf.shape[0]), BF16)
    place_f[...] = jnp.concatenate([one_f, pad], axis=1)
    place_b[...] = jnp.concatenate([one_b, pad], axis=1)
    ship_f[...] = xf[...]
    ship_b[...] = grad[...]


def merge_rows(blocks, used, total):
    d = blocks[0].shape[1]
    stacked = jnp.concatenate([b[...] for b in blocks], axis=0)
    shape = (3 * total, 4 * GATH)
    row, col = iota(shape, 0), iota(shape, 1)
    pick = jnp.zeros(shape, F32)
    for k in range(3):
        for j in range(4):
            local = row - total * k - used * j
            good = (local >= 0) & (local < used) & (col == local + GATH * j + used * k)
            pick = jnp.where(good, 1.0, pick)
    moved = mm(pick.astype(BF16), stacked).astype(BF16)
    return [moved[total * k : total * (k + 1)] for k in range(3)], d


def merge_kernel(a0, a1, a2, a3, b0, b1, b2, b3, big_a, big_b):
    parts, d = merge_rows((a0, a1, a2, a3), N_A, ROWS_A)
    for k in range(3):
        big_a[:, k * d : (k + 1) * d] = parts[k]
    parts, d = merge_rows((b0, b1, b2, b3), N_B, ROWS_B)
    for k in range(3):
        big_b[:, k * d : (k + 1) * d] = parts[k]


def flip_kernel(up_own, up_other, down_own, down_other, after_merge, up, dn):
    half = up_own.shape[1]
    up[:half] = up_own[...].T
    up[half:] = up_other[...].T
    dn[:half] = down_own[...]
    dn[half:] = down_other[...]


def down_kernel(counts, hid, pg, dn, up, *refs):
    blocks = refs[len(refs) - len(counts) :]
    hidden, grad = hid[...], pg[...]
    tile = 768
    for t in range(0, dn.shape[1], tile):
        columns = slice(t, t + tile)
        first = mm(hidden, dn[:, columns])
        second = mm(grad, up[:, columns])
        start = 0
        for block in blocks:
            rows = block.shape[0] // 2
            block[:rows, columns] = first[start : start + rows].astype(BF16)
            block[rows:, columns] = second[start : start + rows].astype(BF16)
            start += rows


def down(hidden, pgrad, dn, up, counts, *others, shape=out):
    d = dn.shape[1]
    kernel = functools.partial(down_kernel, counts)
    shapes = [shape((2 * n, d), BF16) for n in counts]
    return call(kernel, shapes, "down", after=(4 + len(others), len(others)))(
        hidden, pgrad, dn, up, *others
    )


def sum_rows(blocks, used, total):
    acc = blocks[0][...].astype(F32)
    for b in blocks[1:]:
        acc = acc + b[...].astype(F32)
    shape = (4 * SLOTS, 2 * total)
    row, col = iota(shape, 0), iota(shape, 1)
    pick = jnp.zeros(shape, F32)
    for j in range(4):
        for k in range(2):
            slot = row - SLOTS * j - PAD * k
            good = (slot >= 0) & (slot < used) & (col == slot + used * j + total * k)
            pick = jnp.where(good, 1.0, pick)
    moved = mm(pick.astype(BF16), acc.astype(BF16)).astype(BF16)
    return [moved[SLOTS * j : SLOTS * (j + 1)] for j in range(4)]


def sum_kernel(a0, a1, a2, a3, b0, b1, b2, b3, their_up, their_down, *outs):
    parts = sum_rows((a0, a1, a2, a3), N_A, ROWS_A) + sum_rows((b0, b1, b2, b3), N_B, ROWS_B)
    for ref, part in zip(outs, parts):
        ref[...] = part


def rows_kernel(
    a0, a1, a2, a3, b0, b1, b2, b3, keep_f, keep_x, keep_g, keep_w, place_f, place_b, gain, y_rows, dx_rows
):
    d = keep_f.shape[1]

    def total(refs):
        acc = refs[0][...].astype(F32)
        for r in refs[1:]:
            acc = acc + r[...].astype(F32)
        return acc.astype(BF16).astype(F32)

    part_a, part_b = total((a0, a1, a2, a3)), total((b0, b1, b2, b3))
    expert = jnp.concatenate([part_a[:PAD], part_b[:PAD]], axis=0)
    du = jnp.concatenate([part_a[PAD:], part_b[PAD:]], axis=0)
    y = keep_f[...].astype(F32) + keep_w[:, 0:1] * expert
    y_rows[:, :d] = y.astype(BF16)
    y_rows[:, d:] = place_f[...]
    x = keep_x[...].astype(F32)
    scale = lax.rsqrt(jnp.mean(x * x, axis=-1, keepdims=True) + EPS)
    h = du * gain[...]
    inner = jnp.mean(h * x, axis=-1, keepdims=True)
    dx = scale * h - x * (scale * scale * scale * inner)
    dx_rows[:, :d] = (keep_g[...].astype(F32) + dx).astype(BF16)
    dx_rows[:, d:] = place_b[...]


def place_kernel(base_f, y_rows, base_b, dx_rows, after_up, after_down, y_out, dx_out):
    tokens, d = base_f.shape
    ones = jnp.ones((SLOTS, 128), BF16)
    for base, rows, result in ((base_f, y_rows, y_out), (base_b, dx_rows, dx_out)):
        chosen = rows[:, d:]
        hit = mm(chosen, ones, ((0,), (0,)))[:tokens, 0:1]
        placed = mm(chosen, rows[:, :d], ((0,), (0,)))[:tokens]
        result[...] = jnp.where(hit > 0.5, placed, base[...].astype(F32)).astype(BF16)


def both(own_a, a, a_axis, own_b, b, b_axis, sign, wait=None):
    a1, a3 = shift(a[0], a_axis, sign), shift(a[2], a_axis, -sign)
    b1, b3 = shift(b[0], b_axis, sign), shift(b[2], b_axis, -sign)
    a2, b2 = a[1], b[1]
    if wait == "a":
        [a2] = after((a2,), (a1,))
    a2, b2 = shift(a2, a_axis, 2), shift(b2, b_axis, 2)
    return [own_a, a1, a2, a3], [own_b, b1, b2, b3]


def ring_gather(own, axis, first):
    ahead = shift(own, axis, 1)
    behind = shift(own, axis, -1)
    return [own, ahead, behind], [shift(ahead[:first], axis, 1), shift(behind[first:], axis, -1)]


def work(blocks, up, dn):
    rows = jnp.concatenate(blocks, axis=0)
    d = up.shape[1]
    rows_a, rows_b, grid_b = rows[:, :d], rows[:, d : 2 * d], rows[:, 2 * d :]
    pre_a = mm(rows_a, up, ((1,), (1,)))
    hidden_a = (pre_a * jax.nn.sigmoid(pre_a)).astype(BF16)
    pre_b = mm(rows_b, up, ((1,), (1,)))
    sigma = jax.nn.sigmoid(pre_b)
    hidden_b = (pre_b * sigma).astype(BF16)
    hidden_grad = mm(grid_b, dn, ((1,), (1,)))
    pgrad = (hidden_grad * sigma * (1.0 + pre_b * (1.0 - sigma))).astype(BF16)
    return hidden_a, (rows_b, grid_b, hidden_b, pgrad)


def on_device(
    fwd_in, fwd_ids, fwd_gate, bwd_in, bwd_ids, bwd_gate, bwd_grad, norm_gain, w_up, w_down
):
    tokens, d = fwd_in.shape[1:]
    send_a, send_b, keep_f, keep_x, keep_g, keep_w, place_f, place_b, base_f, base_b, own_a, own_b = call(
        pack_kernel,
        [pltpu.HBM((GATH, d), BF16)] * 2 + [out((SLOTS, d))] * 3 + [out((SLOTS, 128), F32)] + [out((SLOTS, 128))] * 2
        + [pltpu.HBM((tokens, d), BF16)] * 2 + [out((GATH, d))] * 2,
        "pack",
        62,
    )(
        fwd_in[0],
        fwd_ids[0].T,
        fwd_gate[0].T,
        bwd_in[0],
        bwd_ids[0].T,
        bwd_gate[0].T,
        bwd_grad[0],
        norm_gain,
    )
    up_own, down_own = w_up[0], w_down[0]
    half = up_own.shape[1]
    up_other, down_other = shift(up_own, "core", 1), shift(down_own, "core", 1)
    send_a, send_b = after((send_a, send_b), (up_other, down_other))
    a_blocks, b_blocks = both(own_a, [send_a] * 3, "x", own_b, [send_b] * 3, "y", 1)
    big_a, big_b = call(merge_kernel, [out((ROWS_A, 3 * d)), out((ROWS_B, 3 * d))], "merge")(
        *a_blocks, *b_blocks
    )
    [base_f] = after((base_f,), (big_a,))
    base_f = shift(base_f, "pipe", 1)
    [base_b] = after((base_b,), (base_f,))
    base_b = shift(base_b, "pipe", -1)
    up, dn = call(flip_kernel, [out((2 * half, d))] * 2, "flip", after=(5, 1))(
        up_own, up_other, down_own, down_other, big_a
    )

    near_a, far_a = ring_gather(big_a, "y", 32)
    near_b, far_b = ring_gather(big_b, "x", 24)
    up, dn = after((up, dn), (far_b[0],), hbm=False)
    hidden_near, saved_near = work(near_a + near_b, up, dn)
    near = down(hidden_near, saved_near[3], dn, up, [ROWS_A] * 3 + [ROWS_B] * 3, base_f, base_b, far_b[1])
    hidden_far, saved_far = work(far_a + far_b, up, dn)
    far = down(hidden_far, saved_far[3], dn, up, [ROWS_A, ROWS_B], shape=pltpu.HBM)

    a_sums, b_sums = both(
        near[0], (near[1], far[0], near[2]), "y", near[3], (near[4], far[1], near[5]), "x", -1, "a"
    )
    saved_far = (*saved_far[:2], *after(saved_far[2:], (a_sums[1],), left=(far[0],)))
    over_rows = ((0,), (0,))

    def down_grad(saved, columns):
        return mm(saved[2][:, columns], saved[1], over_rows)

    def up_grad(saved, columns):
        return mm(saved[0], saved[3][:, columns], over_rows)

    theirs, mine = slice(half, None), slice(0, half)
    down_theirs = (down_grad(saved_near, theirs) + down_grad(saved_far, theirs)).astype(BF16)
    up_theirs = (up_grad(saved_near, theirs) + up_grad(saved_far, theirs)).astype(BF16)
    q = call(sum_kernel, [out((SLOTS, d))] * 8, "sums", after=(10, 2))(
        *a_sums, *b_sums, up_theirs, down_theirs
    )
    a_last, b_last = both(q[0], q[1:4], "x", q[4], q[5:8], "y", -1)
    y_rows, dx_rows = call(rows_kernel, [out((SLOTS, d + 128))] * 2, "rows")(
        *a_last, *b_last, keep_f, keep_x, keep_g, keep_w, place_f, place_b, norm_gain
    )
    up_theirs, down_theirs = after((up_theirs, down_theirs), (y_rows,))
    up_theirs, down_theirs = shift(up_theirs, "core", 1), shift(down_theirs, "core", 1)
    saved_far = (*saved_far[:2], *after(saved_far[2:], (up_theirs,), hbm=False))
    down_mine, up_mine = down_grad(saved_far, mine), up_grad(saved_far, mine)
    grad_down = (down_grad(saved_near, mine) + down_mine + down_theirs.astype(F32)).astype(BF16)
    grad_up = (up_grad(saved_near, mine) + up_mine + up_theirs.astype(F32)).astype(BF16)
    y_arrived = shift(y_rows, "pipe", 1)
    dx_arrived = shift(dx_rows, "pipe", -1)
    fwd_out, bwd_out = call(place_kernel, [out((tokens, d)), out((tokens, d))], "place", after=(6, 2))(
        base_f, y_arrived, base_b, dx_arrived, grad_up, grad_down
    )
    return (fwd_out[None], bwd_out[None], grad_up[None], grad_down[None])


def solution(mesh):
    chips = Mesh(mesh.devices.reshape(8, 4, 4, 2), ("pipe", "x", "y", "core"))
    expert = ("x", "y", "core")
    tokens = P("pipe", expert, None)
    return jax.shard_map(
        on_device,
        mesh=chips,
        in_specs=(tokens,) * 7 + (P("pipe", None), P("pipe", None, expert), P("pipe", expert, None)),
        out_specs=(tokens, tokens, P("pipe", None, expert), P("pipe", expert, None)),
        check_vma=False,
    )
```
